128 devices in a mesh: ex: 16 (over y_hi, z, core), ey: 8 (over y_lo, x).
Axes of the slice: x: 4, y: 4 (y_hi: 2, y_lo: 2; y = y_hi * 2 + y_lo), z: 4, core: 2. Of those that a mesh axis runs over, the one named last changes fastest.
Arguments:
- tokens: bfloat16 [32768, 1536], P(('ex', 'ey')), may hold values from -6 to 6
- upstream: bfloat16 [32768, 1536], P(('ex', 'ey')), may hold values from -6 to 6
- route_one: int32 [32768, 1], P(('ex', 'ey')), may hold values from 0 to 15; in each aligned block of 256 rows (0 to 255, 256 to 511, ...) at most 32 rows name the same one
- route_two: int32 [32768, 1], P(('ex', 'ey')), may hold values from 0 to 63; in each aligned block of 256 rows (0 to 255, 256 to 511, ...) at most 8 rows name the same one
- keep_one: int32 [32768], P(('ex', 'ey')), may hold values 0 or 1
- keep_two: int32 [32768], P(('ex', 'ey')), may hold values 0 or 1
- gate_one: float32 [32768, 1], P(('ex', 'ey')), may hold values from 0.25 to 1
- gate_two: float32 [32768, 1], P(('ex', 'ey')), may hold values from 0.25 to 1
- up_one: bfloat16 [16, 1536, 1536], P('ex'), may hold values from -0.15625 to 0.15625
- down_one: bfloat16 [16, 1536, 1536], P('ex'), may hold values from -0.15625 to 0.15625
- up_two: bfloat16 [128, 1536, 768], P(('ex', 'ey')), may hold values from -0.15625 to 0.15625
- down_two: bfloat16 [128, 768, 1536], P(('ex', 'ey')), may hold values from -0.15625 to 0.15625
Outputs:
- result: bfloat16 [32768, 1536], P(('ex', 'ey'))
- grad_tokens: bfloat16 [32768, 1536], P(('ex', 'ey'))
- grad_up_one: bfloat16 [16, 1536, 1536], P('ex', 'ey')
- grad_down_one: bfloat16 [16, 1536, 1536], P('ex', 'ey')
- grad_up_two: bfloat16 [128, 1536, 768], P(('ex', 'ey'))
- grad_down_two: bfloat16 [128, 768, 1536], P(('ex', 'ey'))
The draws below stay inside these ranges and needn't reach their ends.
Inputs may be any that keep to these rules, and one draw needn't show every extreme that they name: `route_one`: in every aligned block of 256 tokens no expert is named more than 32 times, a bound that some block reaches. `route_two`: in every aligned block of 256 tokens no expert is named more than 8 times, a bound that some block reaches.
All inputs are finite; a program needn't handle non-finite values. No bound on the sum of `keep_one` or of `keep_two` on one device may be relied on, other than what follows from the above.
Results may differ from the reference program's by a relative error of at most 0.02.
Values may be sent and summed in bfloat16 or wider, within the bound.
No kernel may reach another device: no remote copies, remote signals or barrier semaphores. Data moves between devices by JAX's collectives and lax.ppermute only.
A program may use at most 128 MiB of HBM per device.

```python
import math
import jax
import jax.numpy as jnp
import numpy as np
from jax import lax

D = 1536
H = 1536
HALF = 768
TOK_DEV = 256
TOKENS = 32768
E1 = 16
E2 = 64
CAP1 = 32
CAP2 = 8
N_EX = 16
N_EY = 8
DEVICES = 128


def with_ends(array, key, least, top_value):
    shape = array.shape
    place = [jax.random.randint(jax.random.fold_in(key, axis), (), 0, shape[axis]) for axis in range(len(shape))]
    array = array.at[tuple(place)].set(least)
    longest = shape.index(max(shape))
    place[longest] = (place[longest] + 1) % shape[longest]
    return array.at[tuple(place)].set(top_value)


def shard_levels(key, shape, split, least, high):
    def one(dim, blocks):
        draws = jax.random.uniform(jax.random.fold_in(jax.random.fold_in(key, 6), dim), (blocks,), jnp.float32, least / len(split), high / len(split))
        return jnp.repeat(jnp.exp(draws), shape[dim] // blocks).reshape((-1,) + (1,) * (len(shape) - dim - 1))

    loudness = one(*split[0])
    for cut in split[1:]:
        loudness = loudness * one(*cut)
    return loudness


def routed_block(stream_key, own, number, rows, number_of, top, limit, lean):
    sequence = jax.random.permutation(stream_key, number_of)
    crowded, usual = shares(number_of, rows * top, limit, lean, True), shares(number_of, rows * top, limit, lean, False)
    places = jnp.arange(number_of)

    def named(sizes, offset_by):
        used = int((sizes > 0).sum())
        fixed = max(1, used // 4)
        moved = fixed + (places - fixed + offset_by * (used - fixed)) % max(1, number_of - fixed)
        return jnp.zeros((number_of,), jnp.int32).at[sequence[jnp.where(places < fixed, places, moved)]].set(jnp.asarray(sizes, jnp.int32))

    sizes = jnp.where(number % 4 == 0, named(crowded, number // 4), named(usual, number - number // 4 - 1))
    mixed = jax.random.permutation(jax.random.fold_in(own, 3), number_of)
    source_of, sink = mixed[0:number_of // 2 * 2:2], mixed[1:number_of // 2 * 2:2]
    margin = jnp.minimum(sizes[source_of] - 1, limit - sizes[sink]) // 2
    margin = jnp.where((source_of == sequence[0]) | (sink == sequence[0]) | (sizes[sink] == 0), 0, jnp.maximum(margin, 0))
    moved = jax.random.randint(jax.random.fold_in(own, 4), (number_of // 2,), 0, 1 << 20) % (margin + 1)
    sizes = sizes.at[source_of].add(-moved).at[sink].add(moved)
    labels = jnp.searchsorted(jnp.cumsum(sizes), jnp.arange(rows * top), side="right").astype(jnp.int32)
    grid = labels.reshape(top, rows).T
    grid = grid[jax.random.permutation(jax.random.fold_in(own, 1), rows)]
    offset_by = jax.random.randint(jax.random.fold_in(own, 2), (rows, 1), 0, top)
    return jnp.take_along_axis(grid, (jnp.arange(top)[None, :] + offset_by) % top, axis=1)


def shares(number_of, total, bound, lean, full):
    loads = [(1 << 20) // math.isqrt(grade ** lean) + 1 for grade in range(1, number_of + 1)]
    largest = bound if full else min(bound, max(-(-total // number_of), total * loads[0] // sum(loads)))
    least = 1 if total - largest >= number_of - 1 else 0
    counts, rest = [largest] + [least] * (number_of - 1), total - largest - least * (number_of - 1)
    while rest > 0:
        movable = [i for i in range(1, number_of) if counts[i] < largest] or [i for i in range(1, number_of) if counts[i] < bound]
        mass, left = sum([loads[i] for i in movable]), rest
        for i in movable:
            extra = min(bound - counts[i], max(1, left * loads[i] // mass), rest)
            counts[i] = counts[i] + extra
            rest = rest - extra
    return np.array(counts)


def gaussian(key, shape, scale, bound, cuts=(), held_as=jnp.bfloat16):
    drawn = jax.random.normal(key, shape, jnp.float32) * scale
    if len(cuts) > 0:
        drawn = shard_levels(key, shape, cuts, -0.22, 0.18) * drawn
    return jnp.clip(drawn, min=-bound, max=bound).astype(held_as)


def setup_inputs(seed: int = 0) -> dict:
    arg_keys = jax.random.split(jax.random.key(seed), 13)
    tokens = gaussian(arg_keys[0], (TOKENS, D), 1.0, 6.0, ((0, 128),))
    upstream = gaussian(arg_keys[1], (TOKENS, D), 1.0, 6.0, ((0, 128),))
    route_one_keys = jax.random.split(jax.random.fold_in(arg_keys[2], 1), TOKENS // TOK_DEV)
    route_one_turns = jax.random.permutation(jax.random.fold_in(arg_keys[2], 3), TOKENS // TOK_DEV)
    route_one = jax.vmap(lambda own, number: routed_block(jax.random.fold_in(arg_keys[2], 2), own, number, TOK_DEV, E1, 1, CAP1, 1))(route_one_keys, route_one_turns).reshape((TOKENS, 1))
    route_two_keys = jax.random.split(jax.random.fold_in(arg_keys[3], 1), TOKENS // TOK_DEV)
    route_two_turns = jax.random.permutation(jax.random.fold_in(arg_keys[3], 3), TOKENS // TOK_DEV)
    route_two = jax.vmap(lambda own, number: routed_block(jax.random.fold_in(arg_keys[3], 2), own, number, TOK_DEV, E2, 1, CAP2, 1))(route_two_keys, route_two_turns).reshape((TOKENS, 1))
    keep_one = with_ends((jax.random.randint(arg_keys[4], (TOKENS,), 0, 8) < 7).astype(jnp.int32), jax.random.fold_in(arg_keys[4], 1), 0, 1)
    keep_two = with_ends((jax.random.randint(arg_keys[5], (TOKENS,), 0, 8) < 7).astype(jnp.int32), jax.random.fold_in(arg_keys[5], 1), 0, 1)
    gate_one = jnp.clip(jnp.exp(math.log(1.0) - 1.3862944 * jax.random.uniform(arg_keys[6], (TOKENS, 1), jnp.float32) ** shard_levels(arg_keys[6], (TOKENS, 1), ((0, 128),), -0.2, 0.2)), 0.25, 1.0)
    gate_two = jnp.clip(jnp.exp(math.log(1.0) - 1.3862944 * jax.random.uniform(arg_keys[7], (TOKENS, 1), jnp.float32) ** shard_levels(arg_keys[7], (TOKENS, 1), ((0, 128),), -0.2, 0.2)), 0.25, 1.0)
    up_one = gaussian(arg_keys[8], (E1, D, H), D ** -0.5, 0.15625, ((0, 16),))
    down_one = gaussian(arg_keys[9], (E1, H, D), H ** -0.5, 0.15625, ((0, 16),))
    up_two = gaussian(arg_keys[10], (2 * E2, D, HALF), D ** -0.5, 0.15625, ((0, 128),))
    down_two = gaussian(arg_keys[11], (2 * E2, HALF, D), H ** -0.5, 0.15625, ((0, 128),))
    return dict(tokens=tokens, upstream=upstream, route_one=route_one, route_two=route_two, keep_one=keep_one, keep_two=keep_two, gate_one=gate_one, gate_two=gate_two, up_one=up_one, down_one=down_one, up_two=up_two, down_two=down_two)


EPS = 1e-06

def rms_scale(values):
    widened = values.astype(jnp.float32)
    return lax.rsqrt(lax.optimization_barrier(jnp.mean(widened * widened, axis=-1, keepdims=True)) + EPS)

def rms_normed(values):
    return (values.astype(jnp.float32) * rms_scale(values)).astype(jnp.bfloat16)

def rms_back(values, incoming):
    inv_rms = rms_scale(values)
    normed = values.astype(jnp.float32) * inv_rms
    grad_in = incoming.astype(jnp.float32)
    return inv_rms * (grad_in - normed * lax.optimization_barrier(jnp.mean(grad_in * normed, axis=-1, keepdims=True)))

def silu_slope(preact):
    sigmoid_value = jax.nn.sigmoid(preact)
    return sigmoid_value * (1.0 + preact * (1.0 - sigmoid_value))

def product(left_side, right_side):
    return jnp.dot(left_side, right_side, preferred_element_type=jnp.float32)

def product_back(left_side, right_side):
    return lax.dot_general(left_side, right_side, (((1,), (1,)), ((), ())), preferred_element_type=jnp.float32)

def product_rows(left_side, right_side):
    return lax.dot_general(left_side, right_side, (((0,), (0,)), ((), ())), preferred_element_type=jnp.float32)

def destinations(route, keep, experts, capacity):
    chosen = route[:, 0].reshape(DEVICES, TOK_DEV)
    onehot = (chosen[:, :, None] == jnp.arange(experts, dtype=jnp.int32)[None, None, :]).astype(jnp.int32)
    before = jnp.cumsum(onehot, axis=1) - onehot
    slot_rank = lax.optimization_barrier(jnp.sum(before * onehot, axis=2))
    device = jnp.arange(DEVICES, dtype=jnp.int32)[:, None]
    target = chosen * (DEVICES * capacity) + device * capacity + slot_rank
    kept_rows = keep.reshape(DEVICES, TOK_DEV) > 0
    return jnp.where(kept_rows, target, experts * DEVICES * capacity).reshape(-1).astype(jnp.int32)

def scatter_rows(values, target, experts, capacity):
    slot_total = experts * DEVICES * capacity
    filled = jnp.zeros((slot_total, D), values.dtype).at[target].set(values, mode='drop')
    return filled.reshape(experts, DEVICES * capacity, D)

def collect_rows(filled, target):
    return jnp.take(filled.reshape(-1, D), target, axis=0, mode='fill', fill_value=0)

def layer_one_forward(packed):
    slot_rows, up_mat, down_mat = packed
    preact = product(slot_rows, up_mat)
    hidden = jax.nn.silu(preact).astype(jnp.bfloat16)
    return (preact, hidden, product(hidden, down_mat).astype(jnp.bfloat16))

def layer_two_forward(packed):
    slot_rows, up_pair, down_pair = packed
    preacts = []
    hiddens = []
    partials = []
    for member in range(2):
        preact = product(slot_rows, up_pair[member])
        hidden = jax.nn.silu(preact).astype(jnp.bfloat16)
        preacts.append(preact)
        hiddens.append(hidden)
        partials.append(product(hidden, down_pair[member]).astype(jnp.bfloat16))
    summed = (partials[0].astype(jnp.float32) + partials[1].astype(jnp.float32)).astype(jnp.bfloat16)
    return (jnp.stack(preacts), jnp.stack(hiddens), summed)

def layer_two_back(packed):
    slot_rows, preacts, hiddens, grad_rows, up_pair, down_pair = packed
    partials = []
    grad_ups = []
    grad_downs = []
    for member in range(2):
        hidden_grad = (product_back(grad_rows, down_pair[member]) * silu_slope(preacts[member])).astype(jnp.bfloat16)
        partials.append(product_back(hidden_grad, up_pair[member]).astype(jnp.bfloat16))
        grad_ups.append(product_rows(slot_rows, hidden_grad).astype(jnp.bfloat16))
        grad_downs.append(product_rows(hiddens[member], grad_rows).astype(jnp.bfloat16))
    summed = (partials[0].astype(jnp.float32) + partials[1].astype(jnp.float32)).astype(jnp.bfloat16)
    return (summed, jnp.stack(grad_ups), jnp.stack(grad_downs))

def layer_one_back(packed):
    slot_rows, preact, hidden, grad_rows, up_mat, down_mat = packed
    hidden_grad = (product_back(grad_rows, down_mat) * silu_slope(preact)).astype(jnp.bfloat16)
    returned = product_back(hidden_grad, up_mat).astype(jnp.bfloat16)
    rows_grouped = slot_rows.reshape(N_EX, N_EY, CAP1, D).astype(jnp.float32)
    inner_grouped = hidden_grad.reshape(N_EX, N_EY, CAP1, H).astype(jnp.float32)
    hidden_grouped = hidden.reshape(N_EX, N_EY, CAP1, H).astype(jnp.float32)
    grads_grouped = grad_rows.reshape(N_EX, N_EY, CAP1, D).astype(jnp.float32)
    term_up = jnp.einsum('xjcd,xjch->jdh', rows_grouped, inner_grouped, precision=lax.Precision.HIGHEST)
    term_down = jnp.einsum('xjch,xjcd->jhd', hidden_grouped, grads_grouped, precision=lax.Precision.HIGHEST)
    term_up = lax.optimization_barrier(term_up.astype(jnp.bfloat16))
    term_down = lax.optimization_barrier(term_down.astype(jnp.bfloat16))
    grad_up = lax.optimization_barrier(jnp.sum(term_up.astype(jnp.float32), axis=0)).astype(jnp.bfloat16)
    grad_down = lax.optimization_barrier(jnp.sum(term_down.astype(jnp.float32), axis=0)).astype(jnp.bfloat16)
    return (returned, grad_up, grad_down)

def reference(tokens, upstream, route_one, route_two, keep_one, keep_two, gate_one, gate_two, up_one, down_one, up_two, down_two):
    target_one = destinations(route_one, keep_one, E1, CAP1)
    target_two = destinations(route_two, keep_two, E2, CAP2)
    rows_one = scatter_rows(rms_normed(tokens), target_one, E1, CAP1)
    pre_one, hidden_one, out_one = lax.map(layer_one_forward, (rows_one, up_one, down_one))
    middle = (tokens.astype(jnp.float32) + gate_one * collect_rows(out_one, target_one).astype(jnp.float32)).astype(jnp.bfloat16)
    rows_two = scatter_rows(rms_normed(middle), target_two, E2, CAP2)
    ups_two = up_two.reshape(E2, 2, D, HALF)
    downs_two = down_two.reshape(E2, 2, HALF, D)
    pre_two, hidden_two, out_two = lax.map(layer_two_forward, (rows_two, ups_two, downs_two))
    result = (middle.astype(jnp.float32) + gate_two * collect_rows(out_two, target_two).astype(jnp.float32)).astype(jnp.bfloat16)
    send_two = (gate_two * upstream.astype(jnp.float32)).astype(jnp.bfloat16)
    grads_two = scatter_rows(send_two, target_two, E2, CAP2)
    back_two, grad_up_two, grad_down_two = lax.map(layer_two_back, (rows_two, pre_two, hidden_two, grads_two, ups_two, downs_two))
    grad_middle = (upstream.astype(jnp.float32) + rms_back(middle, collect_rows(back_two, target_two))).astype(jnp.bfloat16)
    send_one = (gate_one * grad_middle.astype(jnp.float32)).astype(jnp.bfloat16)
    grads_one = scatter_rows(send_one, target_one, E1, CAP1)
    back_one, grad_up_one, grad_down_one = lax.map(layer_one_back, (rows_one, pre_one, hidden_one, grads_one, up_one, down_one))
    grad_tokens = (grad_middle.astype(jnp.float32) + rms_back(tokens, collect_rows(back_one, target_one))).astype(jnp.bfloat16)
    return (result, grad_tokens, grad_up_one, grad_down_one, grad_up_two.reshape(2 * E2, D, HALF), grad_down_two.reshape(2 * E2, HALF, D))
```

```python
import jax
import jax.numpy as jnp
from jax import lax
from jax.experimental import pallas as pl
from jax.experimental.pallas import tpu as pltpu
from jax.sharding import Mesh
from jax.sharding import PartitionSpec as P

EPS = 1e-06
AXES = ("y_hi", "z", "core", "y_lo", "x")
EX = ("y_hi", "z", "core")
EY = ("y_lo", "x")
CHIPS = ("y_hi", "z", "y_lo", "x")
EXPERTS_ONE, CAP_ONE = 16, 32
EXPERTS_TWO, CAP_TWO = 64, 8
BF, F32 = jnp.bfloat16, jnp.float32
CHUNK = 256


def dot(left, right):
    return jnp.dot(left, right, preferred_element_type=F32)


def dot_nt(left, right):
    return lax.dot_general(left, right, (((1,), (1,)), ((), ())), preferred_element_type=F32)


def dot_tn(left, right):
    return lax.dot_general(left, right, (((0,), (0,)), ((), ())), preferred_element_type=F32)


def iota(shape, axis):
    return lax.broadcasted_iota(jnp.int32, shape, axis)


def slot_targets(route, keep, experts, cap, index_of):
    count = route.shape[1]
    chosen = iota((experts, count), 0) == route
    earlier = (iota((count, count), 0) < iota((count, count), 1)).astype(F32).astype(BF)
    before = dot(chosen.astype(F32).astype(BF), earlier)
    rank = jnp.sum(jnp.where(chosen, before, 0.0), axis=0, keepdims=True).astype(jnp.int32)
    return jnp.where(keep > 0, index_of(route) * cap + rank, -1)


def chip_of(expert):
    return (expert // 8) * 8 + (expert % 4) * 2 + (expert // 4) % 2


def column_of(row):
    count = row.shape[1]
    same = iota((count, count), 0) == iota((count, count), 1)
    return jnp.sum(jnp.where(same, row, jnp.zeros_like(row)), axis=1, keepdims=True)


def place_matrix(target, slots):
    return (iota((slots, target.shape[1]), 0) == target).astype(F32).astype(BF)


def collect_matrix(target, slots):
    column = column_of(target.astype(F32)).astype(jnp.int32)
    return (iota((target.shape[1], slots), 1) == column).astype(F32).astype(BF)


def fill(out_ref, target, rows):
    matrix = place_matrix(target, out_ref.shape[0])
    for start in range(0, out_ref.shape[1], CHUNK):
        part = slice(start, start + CHUNK)
        out_ref[:, part] = dot(matrix, rows[:, part]).astype(out_ref.dtype)


def inverse_rms(values):
    return lax.rsqrt(jnp.mean(values * values, axis=-1, keepdims=True) + EPS)


def rms_back(values, grad):
    inv = inverse_rms(values)
    normed = values * inv
    return inv * (grad - normed * jnp.mean(grad * normed, axis=-1, keepdims=True))


def first_kernel(tok, up, route1, keep1, route2, keep2, gate2, rows1, rows2, target1, target2):
    to_one = slot_targets(route1[...], keep1[...], EXPERTS_ONE, CAP_ONE, lambda e: e)
    to_two = slot_targets(route2[...], keep2[...], EXPERTS_TWO, CAP_TWO, chip_of)
    target1[...] = to_one
    target2[...] = to_two
    values = tok[...].astype(F32)
    fill(rows1, to_one, (values * inverse_rms(values)).astype(BF))
    fill(rows2, to_two, (column_of(gate2[...]) * up[...].astype(F32)).astype(BF))


def middle_kernel(tok, returned, target1, target2, gate1, middle, rows2):
    gathered = dot(collect_matrix(target1[...], returned.shape[0]), returned[...])
    mid = (tok[...].astype(F32) + column_of(gate1[...]) * gathered).astype(BF)
    middle[...] = mid
    values = mid.astype(F32)
    fill(rows2, target2[...], (values * inverse_rms(values)).astype(BF))


def turn_kernel(middle, up, returned, target1, target2, gate1, grad_middle, rows1):
    gathered = dot(collect_matrix(target2[...], returned.shape[0]), returned[...])
    grad = (up[...].astype(F32) + rms_back(middle[...].astype(F32), gathered)).astype(BF)
    grad_middle[...] = grad
    fill(rows1, target1[...], (column_of(gate1[...]) * grad.astype(F32)).astype(BF))


def result_kernel(middle, returned, target2, gate2, result):
    gathered = dot(collect_matrix(target2[...], returned.shape[0]), returned[...])
    result[...] = (middle[...].astype(F32) + column_of(gate2[...]) * gathered).astype(BF)


def last_kernel(tok, grad_middle, returned, target1, grad_tokens):
    gathered = dot(collect_matrix(target1[...], returned.shape[0]), returned[...])
    grad_tokens[...] = (
        grad_middle[...].astype(F32) + rms_back(tok[...].astype(F32), gathered)
    ).astype(BF)


def call(kernel, outs, *args):
    moved = sum(a.size * a.dtype.itemsize for a in args)
    return pl.pallas_call(
        kernel,
        out_shape=outs,
        compiler_params=pltpu.CompilerParams(vmem_limit_bytes=32 * 1024 * 1024),
        cost_estimate=pl.CostEstimate(
            flops=2 * 256 * 512 * 1536, bytes_accessed=2 * moved, transcendentals=0
        ),
    )(*args)


def shape(rows, columns, dtype=BF):
    return jax.ShapeDtypeStruct((rows, columns), dtype)


def exchange_one(rows):
    width = rows.shape[1]
    parts = rows.reshape(EXPERTS_ONE, CAP_ONE, width)
    return lax.all_to_all(parts, EX, split_axis=0, concat_axis=0, tiled=True).reshape(-1, width)


def exchange_two(rows):
    width = rows.shape[1]
    parts = rows.reshape(EXPERTS_TWO, CAP_TWO, width)
    return lax.all_to_all(parts, CHIPS, split_axis=0, concat_axis=0, tiled=True).reshape(-1, width)


def swap_pairs(values):
    size = 4
    pairs = []
    for x in range(size):
        if x % 2 == 0:
            pairs += [(x, x), (size + x, x + 1)]
        else:
            pairs += [(x, size + x - 1), (size + x, size + x)]
    return lax.ppermute(values, ("core", "x"), pairs)


def other_core(values):
    return lax.ppermute(values, "core", [(0, 1), (1, 0)])


def silu_slope(preact):
    sigmoid_value = jax.nn.sigmoid(preact)
    return sigmoid_value * (1.0 + preact * (1.0 - sigmoid_value))


def per_device(
    tokens,
    upstream,
    route_one,
    route_two,
    keep_one,
    keep_two,
    gate_one,
    gate_two,
    up_one,
    down_one,
    up_two,
    down_two,
):
    count, width = tokens.shape
    slots_one, slots_two = EXPERTS_ONE * CAP_ONE, EXPERTS_TWO * CAP_TWO
    route_one, route_two, keep_one, keep_two, gate_one, gate_two = (
        v.reshape(1, count) for v in (route_one, route_two, keep_one, keep_two, gate_one, gate_two)
    )
    up_mine = swap_pairs(up_two[0])
    down_mine = swap_pairs(down_two[0])
    up_other = other_core(up_mine)
    down_other = other_core(down_mine)

    filled_one, filled_grads, target_one, target_two = call(
        first_kernel,
        (
            shape(slots_one, width),
            shape(slots_two, width),
            shape(1, count, jnp.int32),
            shape(1, count, jnp.int32),
        ),
        tokens, upstream, route_one, keep_one, route_two, keep_two, gate_two,
    )
    rows_one = exchange_one(filled_one)
    pre_one = dot(rows_one, up_one[0])
    hidden_one = jax.nn.silu(pre_one).astype(BF)
    returned_one = exchange_one(dot(hidden_one, down_one[0]).astype(BF))
    grads_two = exchange_two(filled_grads)

    middle, filled_two = call(
        middle_kernel,
        (shape(count, width), shape(slots_two, width)),
        tokens, returned_one, target_one, target_two, gate_one,
    )
    rows_two = exchange_two(filled_two)
    pre_mine = dot(rows_two, up_mine)
    pre_other = dot(rows_two, up_other)
    inner_mine = (dot_nt(grads_two, down_mine) * silu_slope(pre_mine)).astype(BF)
    inner_other = (dot_nt(grads_two, down_other) * silu_slope(pre_other)).astype(BF)
    back_two = (dot_nt(inner_mine, up_mine) + dot_nt(inner_other, up_other)).astype(BF)
    returned_back = exchange_two(back_two)
    hidden_mine = jax.nn.silu(pre_mine).astype(BF)
    hidden_other = jax.nn.silu(pre_other).astype(BF)
    out_two = (dot(hidden_mine, down_mine) + dot(hidden_other, down_other)).astype(BF)
    returned_out = exchange_two(out_two)
    term_up_two = other_core(dot_tn(rows_two, inner_other).astype(BF))
    term_down_two = other_core(dot_tn(hidden_other, grads_two).astype(BF))
    grad_up_two = swap_pairs((dot_tn(rows_two, inner_mine) + term_up_two.astype(F32)).astype(BF))
    grad_down_two = swap_pairs(
        (dot_tn(hidden_mine, grads_two) + term_down_two.astype(F32)).astype(BF)
    )

    grad_middle, filled_back = call(
        turn_kernel,
        (shape(count, width), shape(slots_one, width)),
        middle, upstream, returned_back, target_one, target_two, gate_one,
    )
    result = call(
        result_kernel, shape(count, width), middle, returned_out, target_two, gate_two
    )
    grads_one = exchange_one(filled_back)
    inner_one = (dot_nt(grads_one, down_one[0]) * silu_slope(pre_one)).astype(BF)
    back_one = dot_nt(inner_one, up_one[0]).astype(BF)
    returned_last = exchange_one(back_one)
    share_down = lax.psum_scatter(
        dot_tn(hidden_one, grads_one).astype(BF), EY, scatter_dimension=0, tiled=True
    )
    share_up = lax.psum_scatter(
        dot_tn(rows_one, inner_one).astype(BF), EY, scatter_dimension=0, tiled=True
    )
    grad_tokens = call(
        last_kernel, shape(count, width), tokens, grad_middle, returned_last, target_one
    )
    return (
        result,
        grad_tokens,
        share_up[None],
        share_down[None],
        grad_up_two[None],
        grad_down_two[None],
    )


def solution(mesh):
    fine = Mesh(mesh.devices.reshape(2, 4, 2, 2, 4), AXES)
    rows = P(AXES, None)
    weights = P(AXES, None, None)
    return jax.shard_map(
        per_device,
        mesh=fine,
        in_specs=(
            rows, rows, rows, rows, P(AXES), P(AXES), rows, rows,
            P(EX, None, None), P(EX, None, None), weights, weights,
        ),
        out_specs=(rows, rows, P(EX, EY, None), P(EX, EY, None), weights, weights),
        check_vma=False,
    )
```

```python
import jax
import jax.numpy as jnp
from jax import lax
from jax.experimental import pallas as pl
from jax.experimental.pallas import tpu as pltpu
from jax.sharding import Mesh
from jax.sharding import PartitionSpec as P

EPS = 1e-06
AXES = ("y_hi", "z", "core", "y_lo", "x")
EX = ("y_hi", "z", "core")
EY = ("y_lo", "x")
CHIPS = ("y_hi", "z", "y_lo", "x")
EXPERTS_ONE, CAP_ONE = 16, 32
EXPERTS_TWO, CAP_TWO = 64, 8
WIDTH, HALF, COUNT, SLOTS = 1536, 768, 256, 512
SHARE = WIDTH // 8
X_COLS = 1024
Y_COLS = WIDTH - X_COLS
BF, F32 = jnp.bfloat16, jnp.float32
CHUNK = 512
CHUNKS = [slice(start, start + CHUNK) for start in range(0, WIDTH, CHUNK)]
MIB = 1024 * 1024


def dot(left, right):
    return jnp.dot(left, right, preferred_element_type=F32)


def dot_nt(left, right):
    return lax.dot_general(left, right, (((1,), (1,)), ((), ())), preferred_element_type=F32)


def dot_tn(left, right):
    return lax.dot_general(left, right, (((0,), (0,)), ((), ())), preferred_element_type=F32)


def shape(rows, columns, dtype=BF):
    return jax.ShapeDtypeStruct((rows, columns), dtype)


def pieces_of(dims, axis, count):
    size = dims[axis] // count
    return [
        tuple(slice(i * size, (i + 1) * size) if d == axis else slice(0, dims[d]) for d in range(2))
        for i in range(count)
    ]


class Arrivals:
    def __init__(self, ahead):
        self.ahead, self.copies, self.begun, self.done = ahead, [], 0, set()

    def wait(self, number):
        while self.begun < min(number + 1 + self.ahead, len(self.copies)):
            self.copies[self.begun].start()
            self.begun += 1
        if number not in self.done:
            self.copies[number].wait()
            self.done.add(number)


class Input:
    def __init__(self, source, target, pieces, sems, arrivals):
        self.ref, self.arrivals, self.numbers = target, arrivals, []
        for piece in pieces:
            number = len(arrivals.copies)
            arrivals.copies.append(
                pltpu.make_async_copy(source.at[piece], target.at[piece], sems.at[number])
            )
            self.numbers.append(number)

    def get(self, upto=None):
        for number in self.numbers if upto is None else self.numbers[: upto + 1]:
            self.arrivals.wait(number)
        return self.ref


class Output:
    def __init__(self, source, target, sems):
        self.ref, self.target, self.sems, self.leaving = source, target, sems, []

    def send(self, rows=slice(None), columns=slice(None)):
        copy = pltpu.make_async_copy(
            self.ref.at[rows, columns], self.target.at[rows, columns], self.sems.at[len(self.leaving)]
        )
        copy.start()
        self.leaving.append(copy)

    def put(self, columns, value):
        self.ref[:, columns] = value.astype(self.ref.dtype)
        self.send(columns=columns)

    def put_all(self, value):
        self.ref[...] = value.astype(self.ref.dtype)
        self.send()


MOST_PIECES = 6


def call(kernel, outs, args, products=0.1, split=(), scratch=(), vmem=24, after=(), free=(), ahead=4):
    split = dict(split)
    pieces = [pieces_of(a.shape, *split.get(i, (0, 1))) for i, a in enumerate(args)]
    in_sems = sum(len(p) for p in pieces)
    inputs, results = len(args), len(outs)

    def body(*refs):
        refs = list(refs)
        sources, refs = refs[:inputs], refs[inputs:]
        refs = refs[len(after):]
        targets, refs = refs[:results], refs[results:]
        held, refs = refs[:inputs], refs[inputs:]
        made, refs = refs[:results], refs[results:]
        arriving, leaving, extra = refs[0], refs[1], refs[2:]
        arrivals = Arrivals(ahead)
        ins = [
            Input(source, target, parts, arriving, arrivals)
            for source, target, parts in zip(sources, held, pieces)
        ]
        while arrivals.begun < min(ahead, len(arrivals.copies)):
            arrivals.copies[arrivals.begun].start()
            arrivals.begun += 1
        sends = [
            Output(source, target, leaving.at[i]) for i, (source, target) in enumerate(zip(made, targets))
        ]
        kernel(ins, sends, *extra)
        for one in ins:
            one.get()
        for one in sends:
            for copy in one.leaving:
                copy.wait()

    moved = sum(a.size * a.dtype.itemsize for a in (*args, *outs))
    hbm = pl.BlockSpec(memory_space=pltpu.MemorySpace.HBM)
    anywhere = pl.BlockSpec(memory_space=pl.ANY)
    in_hbm = [
        a if i in free else pltpu.with_memory_space_constraint(a, pltpu.MemorySpace.HBM)
        for i, a in enumerate(args)
    ]
    return pl.pallas_call(
        body,
        out_shape=tuple(pltpu.MemorySpace.HBM(o.shape, o.dtype) for o in outs),
        in_specs=[anywhere if i in free else hbm for i in range(inputs)]
        + [hbm] * len(after),
        out_specs=tuple([hbm] * results),
        scratch_shapes=[pltpu.VMEM(a.shape, a.dtype) for a in args]
        + [pltpu.VMEM(o.shape, o.dtype) for o in outs]
        + [pltpu.SemaphoreType.DMA((in_sems,)), pltpu.SemaphoreType.DMA((results, MOST_PIECES))]
        + list(scratch),
        compiler_params=pltpu.CompilerParams(vmem_limit_bytes=vmem * MIB),
        cost_estimate=pl.CostEstimate(
            flops=int(products * 2 * SLOTS * WIDTH * WIDTH), bytes_accessed=moved, transcendentals=0
        ),
    )(*in_hbm, *[pltpu.with_memory_space_constraint(a, pltpu.MemorySpace.HBM) for a in after])


def hold(values, after):
    def nothing(*refs):
        del refs

    return pl.pallas_call(
        nothing,
        out_shape=pltpu.MemorySpace.HBM(values.shape, values.dtype),
        in_specs=[pl.BlockSpec(memory_space=pltpu.MemorySpace.HBM)] * (1 + len(after)),
        out_specs=pl.BlockSpec(memory_space=pltpu.MemorySpace.HBM),
        input_output_aliases={0: 0},
        compiler_params=pltpu.CompilerParams(vmem_limit_bytes=MIB),
    )(*[pltpu.with_memory_space_constraint(a, pltpu.MemorySpace.HBM) for a in (values, *after)])


def iota(dims, axis):
    return lax.broadcasted_iota(jnp.int32, dims, axis)


def slot_targets(route, keep, experts, cap, index_of):
    chosen = iota((experts, COUNT), 0) == route
    earlier = (iota((COUNT, COUNT), 0) < iota((COUNT, COUNT), 1)).astype(F32).astype(BF)
    before = dot(chosen.astype(F32).astype(BF), earlier)
    rank = jnp.sum(jnp.where(chosen, before, 0.0), axis=0, keepdims=True).astype(jnp.int32)
    return jnp.where(keep > 0, index_of(route) * cap + rank, -1)


def chip_of(expert):
    return (expert // 8) * 8 + (expert % 4) * 2 + (expert // 4) % 2


def column_of(row):
    same = iota((COUNT, COUNT), 0) == iota((COUNT, COUNT), 1)
    return jnp.sum(jnp.where(same, row, jnp.zeros_like(row)), axis=1, keepdims=True)


def place_matrix(target):
    return (iota((SLOTS, COUNT), 0) == target).astype(F32).astype(BF)


def collect_matrix(target):
    column = column_of(target.astype(F32)).astype(jnp.int32)
    return (iota((COUNT, SLOTS), 1) == column).astype(F32).astype(BF)


def inverse_rms(values):
    return lax.rsqrt(jnp.mean(values * values, axis=-1, keepdims=True) + EPS)


def rms_back(values, grad):
    inv = inverse_rms(values)
    normed = values * inv
    return inv * (grad - normed * jnp.mean(grad * normed, axis=-1, keepdims=True))


def first_kernel(ins, outs):
    route1, keep1, route2, keep2, tokens = ins
    rows1, target1, target2 = outs
    to_one = slot_targets(route1.get()[...], keep1.get()[...], EXPERTS_ONE, CAP_ONE, lambda e: e)
    to_two = slot_targets(route2.get()[...], keep2.get()[...], EXPERTS_TWO, CAP_TWO, chip_of)
    target1.put_all(to_one)
    target2.put_all(to_two)
    matrix = place_matrix(to_one)
    values = tokens.get()[...].astype(F32)
    normed = (values * inverse_rms(values)).astype(BF)
    for part in CHUNKS:
        rows1.put(part, dot(matrix, normed[:, part]))


def middle_kernel(ins, outs):
    target1, target2, gate1, gate2, upstream, returned, tokens = ins
    middle, rows2 = outs
    collect = collect_matrix(target1.get()[...])
    place = place_matrix(target2.get()[...])
    gate = column_of(gate1.get()[...])
    send = (column_of(gate2.get()[...]) * upstream.get()[...].astype(F32)).astype(BF)
    for part in CHUNKS:
        rows2.put(slice(part.start + WIDTH, part.stop + WIDTH), dot(place, send[:, part]))
    gathered = dot(collect, returned.get()[...])
    mid = (tokens.get()[...].astype(F32) + gate * gathered).astype(BF)
    middle.put_all(mid)
    values = mid.astype(F32)
    normed = (values * inverse_rms(values)).astype(BF)
    for part in CHUNKS:
        rows2.put(part, dot(place, normed[:, part]))


def turn_kernel(ins, outs):
    target1, target2, gate1, returned, middle, upstream = ins
    grad_middle, rows1 = outs
    collect = collect_matrix(target2.get()[...])
    place = place_matrix(target1.get()[...])
    gate = column_of(gate1.get()[...])
    gathered = dot(collect, returned.get()[...])
    grad = (
        upstream.get()[...].astype(F32) + rms_back(middle.get()[...].astype(F32), gathered)
    ).astype(BF)
    grad_middle.put_all(grad)
    send = (gate * grad.astype(F32)).astype(BF)
    for part in CHUNKS:
        rows1.put(part, dot(place, send[:, part]))


def result_kernel(ins, outs):
    target2, gate2, returned, middle = ins
    collect = collect_matrix(target2.get()[...])
    gate = column_of(gate2.get()[...])
    gathered = dot(collect, returned.get()[...])
    outs[0].put_all(middle.get()[...].astype(F32) + gate * gathered)


def last_kernel(ins, outs):
    target1, returned, tokens, grad_middle = ins
    collect = collect_matrix(target1.get()[...])
    gathered = dot(collect, returned.get()[...])
    outs[0].put_all(
        grad_middle.get()[...].astype(F32) + rms_back(tokens.get()[...].astype(F32), gathered)
    )


def one_forward(ins, outs):
    rows, up, down = ins
    out, hidden, slope = outs
    rows = rows.get()
    for number, part in enumerate(CHUNKS):
        pre = dot(rows[...], up.get(number)[:, part])
        sigma = jax.nn.sigmoid(pre)
        hidden.put(part, pre * sigma)
        slope.put(part, sigma * (1.0 + pre * (1.0 - sigma)))
    for number, part in enumerate(CHUNKS):
        out.put(part, dot(hidden.ref[...], down.get(number)[:, part]))


def turned_kernel(ins, outs, wide):
    y_lo, x = lax.axis_index("y_lo"), lax.axis_index("x")
    same = (iota((SLOTS, SLOTS), 0) == iota((SLOTS, SLOTS), 1)).astype(F32).astype(BF)
    for source, target in zip(ins, outs):
        wide[...] = dot_tn(source.get()[...], same).astype(BF)
        for j in range(2):
            for k in range(4):
                share = lax.rem(y_lo + j, 2) * 4 + lax.rem(x + k, 4)
                begin = pl.multiple_of(share * SHARE, SHARE)
                here = (j * 4 + k) * SHARE
                target.ref[here : here + SHARE, :] = wide[pl.ds(begin, SHARE), :]
        target.send()


def one_back(ins, outs):
    grads, hidden_t, down, slope, rows_t = ins
    inner, send_y, keep_y, to_next, to_last, add_next, add_last, own = outs
    half = WIDTH // 2

    def term_y(left, right, columns):
        product = dot(left[...], right[:, X_COLS:]).astype(BF)
        for target, rows in ((keep_y, slice(0, half)), (send_y, slice(half, WIDTH))):
            target.ref[:, columns] = product[rows]
            target.send(columns=columns)

    def term_x(left, right, targets):
        product = dot(left[...], right[:, :X_COLS]).astype(BF)
        for k, (target, begin) in enumerate(targets):
            columns = slice(begin, begin + X_COLS)
            for j in range(2):
                source = j * half + k * SHARE
                target.ref[j * SHARE : (j + 1) * SHARE, columns] = product[source : source + SHARE]
            target.send(columns=columns)

    grads = grads.get()
    term_y(hidden_t.get(), grads, slice(0, Y_COLS))
    term_x(hidden_t.get(), grads, ((own, 0), (add_next, 0), (to_next, 0), (to_last, 0)))
    for part in CHUNKS:
        back = dot_nt(grads[...], down.get()[part, :])
        inner.put(part, back * slope.get()[:, part].astype(F32))
    term_y(rows_t.get(), inner.ref, slice(Y_COLS, 2 * Y_COLS))
    term_x(
        rows_t.get(), inner.ref, ((own, X_COLS), (to_next, X_COLS), (to_last, X_COLS), (add_last, 0))
    )


def one_back_rows(ins, outs):
    inner, up = ins
    inner = inner.get()
    for number, part in enumerate(CHUNKS):
        outs[0].put(part, dot_nt(inner[...], up.get(number)[part, :]))


def two_main(ins, outs):
    arrived, up_mine, down_mine, up_other, down_other = ins
    back, hidden, inner = outs
    for number, (up, down) in enumerate(((up_mine, down_mine), (up_other, down_other))):
        part = slice(number * HALF, (number + 1) * HALF)
        pre = dot(arrived.get(0)[:, :WIDTH], up.get()[...])
        sigma = jax.nn.sigmoid(pre)
        grad = dot_nt(arrived.get()[:, WIDTH:], down.get()[...])
        hidden.put(part, pre * sigma)
        inner.put(part, grad * (sigma * (1.0 + pre * (1.0 - sigma))))
    for part in CHUNKS:
        back.put(
            part,
            dot_nt(inner.ref[:, :HALF], up_mine.ref[part, :])
            + dot_nt(inner.ref[:, HALF:], up_other.ref[part, :]),
        )


def two_grads_other(ins, outs):
    arrived, inner, hidden = ins
    term_up, term_down = outs
    term_up.put_all(dot_tn(arrived.get(0)[:, :WIDTH], inner.get()[:, HALF:]))
    term_down.put_all(dot_tn(hidden.get()[:, HALF:], arrived.get()[:, WIDTH:]))


def two_grads_mine(ins, outs):
    arrived, inner, hidden, got_up, got_down = ins
    sum_up, sum_down = outs
    up = dot_tn(arrived.get(0)[:, :WIDTH], inner.get()[:, :HALF])
    sum_up.put_all(up + got_up.get()[...].astype(F32))
    down = dot_tn(hidden.get()[:, :HALF], arrived.get()[:, WIDTH:])
    sum_down.put_all(down + got_down.get()[...].astype(F32))


def two_out(ins, outs):
    hidden, down_mine, down_other = ins
    hidden = hidden.get()
    for part in CHUNKS:
        outs[0].put(
            part,
            dot(hidden[:, :HALF], down_mine.get()[:, part])
            + dot(hidden[:, HALF:], down_other.get()[:, part]),
        )


def total(*parts):
    result = parts[0].astype(F32)
    for part in parts[1:]:
        result = result + part.astype(F32)
    return result


def pass_on(ins, outs):
    add_next, from_last, add_last, from_next = ins
    half = add_next.ref.shape[1]
    outs[0].put_all(total(add_next.get()[...], from_last.get()[:, :half]))
    outs[1].put_all(total(add_last.get()[...], from_next.get()[:, half:]))


def x_sums(ins):
    own, from_next, from_last, more_last, more_next = ins
    half = more_last.ref.shape[1]
    first = total(own.get()[:, :half], from_next.get()[:, :half], more_last.get()[...])
    second = total(own.ref[:, half:], from_last.get()[:, half:], more_next.get()[...])
    return first, second


def first_sums(ins, outs):
    keep, send = outs
    for number, value in enumerate(x_sums(ins)):
        columns = slice(number * X_COLS, (number + 1) * X_COLS)
        keep.put(columns, value[:SHARE])
        send.put(columns, value[SHARE:])


def second_sums(ins, outs):
    keep, got = ins
    to_next, to_last, add_next, add_last, own = outs
    value = total(keep.get()[...], got.get()[...])
    share = [value[k * SHARE : (k + 1) * SHARE] for k in range(4)]
    down, up = slice(0, Y_COLS), slice(Y_COLS, 2 * Y_COLS)
    to_next.put(down, share[2][:, down])
    to_next.put(up, share[1][:, up])
    to_last.put(down, share[3][:, down])
    to_last.put(up, share[2][:, up])
    add_next.put_all(share[1][:, down])
    add_last.put_all(share[3][:, up])
    own.put_all(share[0])


def last_sums(ins, outs):
    keep, got = ins[:2]
    for number, (value, target) in enumerate(zip(x_sums(ins[2:]), outs)):
        columns = slice(number * X_COLS, (number + 1) * X_COLS)
        target.put(slice(0, X_COLS), total(keep.get()[:, columns], got.get()[:, columns]))
        target.put(slice(X_COLS, WIDTH), value)


def exchange_one(rows):
    parts = rows.reshape(EXPERTS_ONE, CAP_ONE, rows.shape[1])
    return lax.all_to_all(parts, EX, split_axis=0, concat_axis=0, tiled=True).reshape(rows.shape)


def exchange_two(rows):
    parts = rows.reshape(EXPERTS_TWO, CAP_TWO, rows.shape[1])
    return lax.all_to_all(parts, CHIPS, split_axis=0, concat_axis=0, tiled=True).reshape(rows.shape)


def swap_pairs(values):
    size = 4
    pairs = []
    for x in range(0, size, 2):
        pairs += [(size + x, x + 1), (x + 1, size + x)]
    return lax.ppermute(values, ("core", "x"), pairs)


def own_or(values, moved):
    stays = lax.axis_index("core") == lax.axis_index("x") % 2
    return jnp.where(stays, values, moved)


def other_core(values):
    return lax.ppermute(values, "core", [(0, 1), (1, 0)])


def other_y(values):
    return lax.ppermute(values, "y_lo", [(0, 1), (1, 0)])


def x_step(values, by):
    return lax.ppermute(values, "x", [(i, (i + by) % 4) for i in range(4)])


def per_device(
    tokens,
    upstream,
    route_one,
    route_two,
    keep_one,
    keep_two,
    gate_one,
    gate_two,
    up_one,
    down_one,
    up_two,
    down_two,
):
    route_one, route_two, keep_one, keep_two, gate_one, gate_two = (
        v.reshape(1, COUNT) for v in (route_one, route_two, keep_one, keep_two, gate_one, gate_two)
    )
    up_one, down_one = up_one[0], down_one[0]
    slots, tall, ints = shape(SLOTS, WIDTH), shape(COUNT, WIDTH), shape(1, COUNT, jnp.int32)

    up_mine = own_or(up_two[0], swap_pairs(up_two[0]))
    down_mine = own_or(down_two[0], swap_pairs(down_two[0]))
    up_other = other_core(up_mine)
    down_other = other_core(down_mine)

    filled_one, target_one, target_two = call(
        first_kernel, (slots, ints, ints), (route_one, keep_one, route_two, keep_two, tokens), ahead=5
    )
    rows_one = exchange_one(filled_one)
    out_one, hidden_one, slope_one = call(
        one_forward, (slots,) * 3, (rows_one, up_one, down_one), 2.2, {1: (1, 3), 2: (1, 3)},
        vmem=32, free=(0,), ahead=1,
    )
    returned_one = exchange_one(out_one)
    turned = shape(WIDTH, SLOTS)
    hidden_t, rows_t = call(
        turned_kernel, (turned, turned), (hidden_one, rows_one), 0.7, vmem=24, free=(1,),
        scratch=[pltpu.VMEM((WIDTH, SLOTS), BF)],
    )

    middle, filled_two = call(
        middle_kernel, (tall, shape(SLOTS, 2 * WIDTH)),
        (target_one, target_two, gate_one, gate_two, upstream, returned_one, tokens), 0.3,
        vmem=24, free=(5,), ahead=7,
    )
    arrived = exchange_two(filled_two)
    back_two, hidden_two, inner_two = call(
        two_main, (slots,) * 3, (arrived, up_mine, down_mine, up_other, down_other), 3.3, {0: (1, 2)},
        vmem=32, free=(0,), ahead=2,
    )
    returned_back = exchange_two(back_two)
    halves = (shape(WIDTH, HALF), shape(HALF, WIDTH))
    term_up, term_down = call(
        two_grads_other, halves, (arrived, inner_two, hidden_two), 1.2, {0: (1, 2)}, vmem=28, free=(0,)
    )
    sum_up, sum_down = call(
        two_grads_mine, halves,
        (arrived, inner_two, hidden_two, other_core(term_up), other_core(term_down)), 1.2, {0: (1, 2)},
        vmem=32, free=(0,),
    )
    moved_up, moved_down = swap_pairs(sum_up), swap_pairs(sum_down)
    grad_up_two, grad_down_two = own_or(sum_up, moved_up), own_or(sum_down, moved_down)
    (out_two,) = call(
        two_out, (slots,), (hidden_two, down_mine, down_other), 1.0, vmem=24, after=(sum_up,)
    )

    grad_middle, filled_back = call(
        turn_kernel, (tall, slots),
        (target_one, target_two, gate_one, returned_back, middle, upstream), 0.3,
        vmem=24, free=(3,), ahead=6, after=(sum_up, sum_down, out_two),
    )
    grads_one = exchange_one(filled_back)
    tall_y = shape(WIDTH // 2, 2 * Y_COLS)
    both, single = shape(2 * SHARE, 2 * X_COLS), shape(2 * SHARE, X_COLS)
    inner_one, send_y, keep_y, to_next, to_last, add_next, add_last, own = call(
        one_back, (slots, tall_y, tall_y, both, both, single, single, both), (grads_one, hidden_t, down_one, slope_one, rows_t),
        3.0, vmem=44, free=(0,), after=(moved_up,), ahead=1,
    )
    returned_out = exchange_two(hold(out_two, (own,)))
    (back_one,) = call(
        one_back_rows, (slots,), (inner_one, up_one), 1.0, {1: (0, 3)}, after=(moved_down,)
    )
    returned_last = exchange_one(hold(back_one, (returned_out,)))

    got_y = other_y(send_y)
    from_last, from_next = x_step(to_next, 1), x_step(to_last, 3)
    on_next, on_last = call(
        pass_on, (single, single), (add_next, from_last, add_last, from_next)
    )
    narrow = shape(SHARE, 2 * X_COLS)
    more_last, more_next = x_step(on_next, 1), x_step(on_last, 3)
    keep, send = call(
        first_sums, (narrow, narrow), (own, from_next, from_last, more_last, more_next)
    )
    got = other_y(send)
    both, single = shape(SHARE, 2 * Y_COLS), shape(SHARE, Y_COLS)
    to_next, to_last, add_next, add_last, own = call(
        second_sums, (both, both, single, single, both), (keep_y, got_y), after=(more_last, more_next)
    )
    from_last, from_next = x_step(to_next, 1), x_step(to_last, 3)
    on_next, on_last = call(
        pass_on, (single, single), (add_next, from_last, add_last, from_next)
    )
    share_down, share_up = call(
        last_sums, (shape(SHARE, WIDTH),) * 2,
        (keep, got, own, from_next, from_last, x_step(on_next, 1), x_step(on_last, 3)),
    )

    (result,) = call(result_kernel, (tall,), (target_two, gate_two, returned_out, middle), free=(2,))
    (grad_tokens,) = call(last_kernel, (tall,), (target_one, returned_last, tokens, grad_middle), free=(1,))
    return (
        result,
        grad_tokens,
        share_up[None],
        share_down[None],
        grad_up_two[None],
        grad_down_two[None],
    )


def solution(mesh):
    fine = Mesh(mesh.devices.reshape(2, 4, 2, 2, 4), AXES)
    rows = P(AXES, None)
    weights = P(AXES, None, None)
    return jax.shard_map(
        per_device,
        mesh=fine,
        in_specs=(
            rows, rows, rows, rows, P(AXES), P(AXES), rows, rows,
            P(EX, None, None), P(EX, None, None), weights, weights,
        ),
        out_specs=(rows, rows, P(EX, EY, None), P(EX, EY, None), weights, weights),
        check_vma=False,
    )
```

```python
import jax
import jax.numpy as jnp
from jax import lax
from jax.experimental import pallas as pl
from jax.experimental.pallas import tpu as pltpu
from jax.sharding import Mesh
from jax.sharding import PartitionSpec as P

EPS = 1e-06
AXES = ("y_hi", "z", "core", "y_lo", "x")
EX = ("y_hi", "z", "core")
EY = ("y_lo", "x")
PAIRED = ("y_hi", "z", "core", "y_lo")
CHIPS = ("y_hi", "z", "y_lo", "x")
EXPERTS_ONE, CAP_ONE = 16, 32
EXPERTS_TWO, CAP_TWO = 64, 8
WIDTH, HALF, COUNT, SLOTS = 1536, 768, 256, 512
SHARE = WIDTH // 8
BF, F32 = jnp.bfloat16, jnp.float32
CHUNK = 512
CHUNKS = [slice(start, start + CHUNK) for start in range(0, WIDTH, CHUNK)]
MIB = 1024 * 1024


def dot(left, right):
    return jnp.dot(left, right, preferred_element_type=F32)


def dot_nt(left, right):
    return lax.dot_general(left, right, (((1,), (1,)), ((), ())), preferred_element_type=F32)


def dot_tn(left, right):
    return lax.dot_general(left, right, (((0,), (0,)), ((), ())), preferred_element_type=F32)


def shape(rows, columns, dtype=BF):
    return jax.ShapeDtypeStruct((rows, columns), dtype)


def pieces_of(dims, axis, count):
    size = dims[axis] // count
    return [
        tuple(slice(i * size, (i + 1) * size) if d == axis else slice(0, dims[d]) for d in range(2))
        for i in range(count)
    ]


class Arrivals:
    def __init__(self, ahead):
        self.ahead, self.copies, self.begun, self.done = ahead, [], 0, set()

    def wait(self, number):
        while self.begun < min(number + 1 + self.ahead, len(self.copies)):
            self.copies[self.begun].start()
            self.begun += 1
        if number not in self.done:
            self.copies[number].wait()
            self.done.add(number)


class Input:
    def __init__(self, source, target, pieces, sems, arrivals):
        self.ref, self.arrivals, self.numbers = target, arrivals, []
        for piece in pieces:
            number = len(arrivals.copies)
            arrivals.copies.append(
                pltpu.make_async_copy(source.at[piece], target.at[piece], sems.at[number])
            )
            self.numbers.append(number)

    def get(self, upto=None):
        for number in self.numbers if upto is None else self.numbers[: upto + 1]:
            self.arrivals.wait(number)
        return self.ref


class Output:
    def __init__(self, source, target, sems):
        self.ref, self.target, self.sems, self.leaving = source, target, sems, []

    def send(self, rows=slice(None), columns=slice(None)):
        copy = pltpu.make_async_copy(
            self.ref.at[rows, columns], self.target.at[rows, columns], self.sems.at[len(self.leaving)]
        )
        copy.start()
        self.leaving.append(copy)

    def put(self, columns, value):
        self.ref[:, columns] = value.astype(self.ref.dtype)
        self.send(columns=columns)

    def put_all(self, value):
        self.ref[...] = value.astype(self.ref.dtype)
        self.send()


MOST_PIECES = 6


def call(kernel, outs, args, products=0.1, split=(), scratch=(), vmem=24, after=(), free=(), ahead=4,
         raw=(), cost=1.0):
    split = dict(split)
    pieces = [pieces_of(a.shape, *split.get(i, (0, 1))) for i, a in enumerate(args)]
    in_sems = sum(len(p) for p in pieces)
    inputs, results = len(args), len(outs)

    def body(*refs):
        refs = list(refs)
        sources, refs = refs[:inputs], refs[inputs:]
        own_work, refs = refs[: len(raw)], refs[len(raw) + len(after) :]
        targets, refs = refs[:results], refs[results:]
        held, refs = refs[:inputs], refs[inputs:]
        made, refs = refs[:results], refs[results:]
        arriving, leaving, extra = refs[0], refs[1], refs[2:]
        arrivals = Arrivals(ahead)
        ins = [
            Input(source, target, parts, arriving, arrivals)
            for source, target, parts in zip(sources, held, pieces)
        ]
        while arrivals.begun < min(ahead, len(arrivals.copies)):
            arrivals.copies[arrivals.begun].start()
            arrivals.begun += 1
        sends = [
            Output(source, target, leaving.at[i]) for i, (source, target) in enumerate(zip(made, targets))
        ]
        kernel(ins, sends, *own_work, *extra)
        for one in ins:
            one.get()
        for one in sends:
            for copy in one.leaving:
                copy.wait()

    moved = sum(a.size * a.dtype.itemsize for a in (*args, *outs))
    hbm = pl.BlockSpec(memory_space=pltpu.MemorySpace.HBM)
    anywhere = pl.BlockSpec(memory_space=pl.ANY)
    in_hbm = [
        a if i in free else pltpu.with_memory_space_constraint(a, pltpu.MemorySpace.HBM)
        for i, a in enumerate(args)
    ]
    return pl.pallas_call(
        body,
        out_shape=tuple(pltpu.MemorySpace.HBM(o.shape, o.dtype) for o in outs),
        in_specs=[anywhere if i in free else hbm for i in range(inputs)]
        + [hbm] * len(raw)
        + [hbm] * len(after),
        out_specs=tuple([hbm] * results),
        scratch_shapes=[pltpu.VMEM(a.shape, a.dtype) for a in args]
        + [pltpu.VMEM(o.shape, o.dtype) for o in outs]
        + [pltpu.SemaphoreType.DMA((in_sems,)), pltpu.SemaphoreType.DMA((results, MOST_PIECES))]
        + list(scratch),
        compiler_params=pltpu.CompilerParams(vmem_limit_bytes=vmem * MIB),
        cost_estimate=pl.CostEstimate(
            flops=int(cost * products * 2 * SLOTS * WIDTH * WIDTH), bytes_accessed=int(cost * moved),
            transcendentals=0,
        ),
    )(*in_hbm, *[pltpu.with_memory_space_constraint(a, pltpu.MemorySpace.HBM) for a in (*raw, *after)])


def hold(values, after):
    def nothing(*refs):
        del refs

    return pl.pallas_call(
        nothing,
        out_shape=pltpu.MemorySpace.HBM(values.shape, values.dtype),
        in_specs=[pl.BlockSpec(memory_space=pltpu.MemorySpace.HBM)]
        + [pl.BlockSpec(memory_space=pl.ANY)] * len(after),
        out_specs=pl.BlockSpec(memory_space=pltpu.MemorySpace.HBM),
        input_output_aliases={0: 0},
        compiler_params=pltpu.CompilerParams(vmem_limit_bytes=MIB),
    )(pltpu.with_memory_space_constraint(values, pltpu.MemorySpace.HBM), *after)


def iota(dims, axis):
    return lax.broadcasted_iota(jnp.int32, dims, axis)


def slot_targets(route, keep, experts, cap, index_of):
    chosen = iota((experts, COUNT), 0) == route
    earlier = (iota((COUNT, COUNT), 0) < iota((COUNT, COUNT), 1)).astype(F32).astype(BF)
    before = dot(chosen.astype(F32).astype(BF), earlier)
    rank = jnp.sum(jnp.where(chosen, before, 0.0), axis=0, keepdims=True).astype(jnp.int32)
    return jnp.where(keep > 0, index_of(route) * cap + rank, -1)


def chip_of(expert):
    return (expert // 8) * 8 + (expert % 4) * 2 + (expert // 4) % 2


def column_of(row):
    same = iota((COUNT, COUNT), 0) == iota((COUNT, COUNT), 1)
    return jnp.sum(jnp.where(same, row, jnp.zeros_like(row)), axis=1, keepdims=True)


def place_matrix(target):
    return (iota((SLOTS, COUNT), 0) == target).astype(F32).astype(BF)


def collect_matrix(target):
    column = column_of(target.astype(F32)).astype(jnp.int32)
    return (iota((COUNT, SLOTS), 1) == column).astype(F32).astype(BF)


def inverse_rms(values):
    return lax.rsqrt(jnp.mean(values * values, axis=-1, keepdims=True) + EPS)


def rms_back(values, grad):
    inv = inverse_rms(values)
    normed = values * inv
    return inv * (grad - normed * jnp.mean(grad * normed, axis=-1, keepdims=True))


def first_kernel(ins, outs):
    route1, keep1, route2, keep2, tokens = ins
    rows1, target1, target2 = outs
    to_one = slot_targets(route1.get()[...], keep1.get()[...], EXPERTS_ONE, CAP_ONE, lambda e: e)
    to_two = slot_targets(route2.get()[...], keep2.get()[...], EXPERTS_TWO, CAP_TWO, chip_of)
    target1.put_all(to_one)
    target2.put_all(to_two)
    matrix = place_matrix(to_one)
    values = tokens.get()[...].astype(F32)
    normed = (values * inverse_rms(values)).astype(BF)
    for part in CHUNKS:
        rows1.put(part, dot(matrix, normed[:, part]))


def middle_kernel(ins, outs):
    target1, target2, gate1, gate2, upstream, returned, tokens = ins
    middle, rows2 = outs
    collect = collect_matrix(target1.get()[...])
    place = place_matrix(target2.get()[...])
    gate = column_of(gate1.get()[...])
    send = (column_of(gate2.get()[...]) * upstream.get()[...].astype(F32)).astype(BF)
    for part in CHUNKS:
        rows2.put(slice(part.start + WIDTH, part.stop + WIDTH), dot(place, send[:, part]))
    gathered = dot(collect, returned.get()[...])
    mid = (tokens.get()[...].astype(F32) + gate * gathered).astype(BF)
    middle.put_all(mid)
    values = mid.astype(F32)
    normed = (values * inverse_rms(values)).astype(BF)
    for part in CHUNKS:
        rows2.put(part, dot(place, normed[:, part]))


def turn_kernel(ins, outs):
    target1, target2, gate1, returned, middle, upstream = ins
    grad_middle, rows1 = outs
    collect = collect_matrix(target2.get()[...])
    row = iota((2 * SLOTS, COUNT), 0)
    slot = row // (2 * CAP_ONE) * CAP_ONE + lax.rem(row, CAP_ONE)
    place = (slot == target1.get()[...]).astype(F32).astype(BF)
    gate = column_of(gate1.get()[...])
    gathered = dot(collect, returned.get()[...])
    grad = (
        upstream.get()[...].astype(F32) + rms_back(middle.get()[...].astype(F32), gathered)
    ).astype(BF)
    grad_middle.put_all(grad)
    send = (gate * grad.astype(F32)).astype(BF)
    for part in CHUNKS:
        rows1.put(part, dot(place, send[:, part]))


def result_kernel(ins, outs):
    target2, gate2, returned, middle = ins
    collect = collect_matrix(target2.get()[...])
    gate = column_of(gate2.get()[...])
    gathered = dot(collect, returned.get()[...])
    outs[0].put_all(middle.get()[...].astype(F32) + gate * gathered)


def last_kernel(ins, outs):
    target1, returned, tokens, grad_middle = ins
    collect = collect_matrix(target1.get()[...])
    gathered = dot(collect, returned.get()[...])
    outs[0].put_all(
        grad_middle.get()[...].astype(F32) + rms_back(tokens.get()[...].astype(F32), gathered)
    )


def one_forward(ins, outs):
    rows, up, down = ins
    out, hidden, slope = outs
    rows = rows.get()
    for number, part in enumerate(CHUNKS):
        pre = dot(rows[...], up.get(number)[:, part])
        sigma = jax.nn.sigmoid(pre)
        hidden.put(part, pre * sigma)
        slope.put(part, sigma * (1.0 + pre * (1.0 - sigma)))
    for number, part in enumerate(CHUNKS):
        out.put(part, dot(hidden.ref[...], down.get(number)[:, part]))


def one_side(ins, outs, hidden_v, own_rows, own_hidden):
    rows, up, first_hidden, first_rows = ins
    slope, hidden_t, rows_t = outs
    y_lo, x = lax.axis_index("y_lo"), lax.axis_index("x")
    rows = rows.get()
    for number, part in enumerate(CHUNKS):
        pre = dot(rows[...], up.get(number)[:, part])
        sigma = jax.nn.sigmoid(pre)
        hidden_v[:, part] = (pre * sigma).astype(BF)
        slope.put(part, sigma * (1.0 + pre * (1.0 - sigma)))
    same = (iota((SLOTS, SLOTS), 0) == iota((SLOTS, SLOTS), 1)).astype(F32).astype(BF)
    columns = pl.ds(pl.multiple_of(y_lo * HALF, HALF), HALF)
    for sources, target, wide in (
        ((first_hidden.get(), hidden_v), hidden_t, own_hidden),
        ((first_rows.get(), rows), rows_t, own_rows),
    ):
        for number, source in enumerate(sources):
            wide[...] = dot_tn(source[:, columns], same).astype(BF)
            for k in range(4):
                begin = pl.multiple_of(lax.rem(x + k, 4) * SHARE, SHARE)
                target.ref[k * SHARE : (k + 1) * SHARE, number * SLOTS : (number + 1) * SLOTS] = (
                    wide[pl.ds(begin, SHARE), :]
                )
        target.send()


def one_back(ins, outs, grads, grads_v, inner_v, sems):
    down, slope, other_slope, hidden_t, rows_t = ins
    inner, to_next, to_last, add_next, add_last, own = outs
    number = lax.rem(lax.axis_index("y_hi") + lax.axis_index("y_lo"), 2)
    half = EXPERTS_ONE // 2
    copies = [
        pltpu.make_async_copy(
            grads.at[y_hi * half : (y_hi + 1) * half, lax.rem(number + y_hi + j, 2)],
            grads_v.at[j, y_hi * half : (y_hi + 1) * half],
            sems.at[2 * j + y_hi],
        )
        for j in range(2)
        for y_hi in range(2)
    ]
    for copy in copies:
        copy.start()
    down.get(0)
    for j, factor in enumerate((slope, other_slope)):
        copies[2 * j].wait()
        copies[2 * j + 1].wait()
        here = slice(j * SLOTS, (j + 1) * SLOTS)
        for number, part in enumerate(CHUNKS):
            back = dot_nt(grads_v[j].reshape(SLOTS, WIDTH), down.get(number)[part, :])
            inner_v[here, part] = (back * factor.get()[:, part].astype(F32)).astype(BF)
            if j == 0:
                inner.put(part, inner_v[here, part])

    def term(left, right, targets):
        for part in CHUNKS:
            product = dot(left[...], right(part)).astype(BF)
            for k, (target, begin) in enumerate(targets):
                columns = slice(begin + part.start, begin + part.stop)
                target.put(columns, product[k * SHARE : (k + 1) * SHARE])

    term(
        hidden_t.get(), lambda part: grads_v[:, :, :, part].reshape(2 * SLOTS, CHUNK),
        ((own, 0), (add_next, 0), (to_next, 0), (to_last, 0)),
    )
    term(
        rows_t.get(), lambda part: inner_v[:, part],
        ((own, WIDTH), (to_next, WIDTH), (to_last, WIDTH), (add_last, 0)),
    )


def one_back_rows(ins, outs):
    inner, up = ins
    inner = inner.get()
    for number, part in enumerate(CHUNKS):
        outs[0].put(part, dot_nt(inner[...], up.get(number)[part, :]))


def two_main(ins, outs):
    arrived, up_mine, down_mine, up_other, down_other = ins
    back, hidden, inner = outs
    for number, (up, down) in enumerate(((up_mine, down_mine), (up_other, down_other))):
        part = slice(number * HALF, (number + 1) * HALF)
        pre = dot(arrived.get(0)[:, :WIDTH], up.get()[...])
        sigma = jax.nn.sigmoid(pre)
        grad = dot_nt(arrived.get()[:, WIDTH:], down.get()[...])
        hidden.put(part, pre * sigma)
        inner.put(part, grad * (sigma * (1.0 + pre * (1.0 - sigma))))
    for part in CHUNKS:
        back.put(
            part,
            dot_nt(inner.ref[:, :HALF], up_mine.ref[part, :])
            + dot_nt(inner.ref[:, HALF:], up_other.ref[part, :]),
        )


def two_grads_other(ins, outs):
    arrived, inner, hidden = ins
    term_up, term_down = outs
    term_up.put_all(dot_tn(arrived.get(0)[:, :WIDTH], inner.get()[:, HALF:]))
    term_down.put_all(dot_tn(hidden.get()[:, HALF:], arrived.get()[:, WIDTH:]))


def two_grads_mine(ins, outs):
    arrived, inner, hidden, got_up, got_down = ins
    sum_up, sum_down = outs
    up = dot_tn(arrived.get(0)[:, :WIDTH], inner.get()[:, :HALF])
    sum_up.put_all(up + got_up.get()[...].astype(F32))
    down = dot_tn(hidden.get()[:, :HALF], arrived.get()[:, WIDTH:])
    sum_down.put_all(down + got_down.get()[...].astype(F32))


def two_out(ins, outs):
    hidden, down_mine, down_other = ins
    hidden = hidden.get()
    for part in CHUNKS:
        outs[0].put(
            part,
            dot(hidden[:, :HALF], down_mine.get()[:, part])
            + dot(hidden[:, HALF:], down_other.get()[:, part]),
        )


def total(*parts):
    result = parts[0].astype(F32)
    for part in parts[1:]:
        result = result + part.astype(F32)
    return result


def pass_on(ins, outs):
    add_next, from_last, add_last, from_next = ins
    half = add_next.ref.shape[1]
    outs[0].put_all(total(add_next.get()[...], from_last.get()[:, :half]))
    outs[1].put_all(total(add_last.get()[...], from_next.get()[:, half:]))


def x_sums(ins):
    own, from_next, from_last, more_last, more_next = ins
    half = more_last.ref.shape[1]
    first = total(own.get()[:, :half], from_next.get()[:, :half], more_last.get()[...])
    second = total(own.ref[:, half:], from_last.get()[:, half:], more_next.get()[...])
    return first, second


def last_sums(ins, outs):
    for value, target in zip(x_sums(ins), outs):
        target.put_all(value)


NEAREST = [
    [
        ((y_hi * 4 + z) * 2 + core) * 2 + (number ^ y_hi)
        for y_hi in range(2)
        for z in range(4)
        for core in range(2)
    ]
    for number in range(2)
]


def exchange_one(rows):
    parts = rows.reshape(EXPERTS_ONE, CAP_ONE, rows.shape[1])
    return lax.all_to_all(
        parts, PAIRED, split_axis=0, concat_axis=0, tiled=True, axis_index_groups=NEAREST
    ).reshape(rows.shape)


def exchange_pairs(rows):
    parts = rows.reshape(2 * EXPERTS_ONE, CAP_ONE, WIDTH)
    parts = lax.all_to_all(parts, PAIRED, split_axis=0, concat_axis=0, tiled=True)
    return parts.reshape(EXPERTS_ONE, 2, CAP_ONE, WIDTH)


def echo(values):
    return other_core(values[:16, :128])


def exchange_two(rows):
    parts = rows.reshape(EXPERTS_TWO, CAP_TWO, rows.shape[1])
    return lax.all_to_all(parts, CHIPS, split_axis=0, concat_axis=0, tiled=True).reshape(rows.shape)


def swap_pairs(values):
    size = 4
    pairs = []
    for x in range(0, size, 2):
        pairs += [(size + x, x + 1), (x + 1, size + x)]
    return lax.ppermute(values, ("core", "x"), pairs)


def own_or(values, moved):
    stays = lax.axis_index("core") == lax.axis_index("x") % 2
    return jnp.where(stays, values, moved)


def other_core(values):
    return lax.ppermute(values, "core", [(0, 1), (1, 0)])


def other_y(values):
    return lax.ppermute(values, "y_lo", [(0, 1), (1, 0)])


def x_step(values, by):
    return lax.ppermute(values, "x", [(i, (i + by) % 4) for i in range(4)])


def per_device(
    tokens,
    upstream,
    route_one,
    route_two,
    keep_one,
    keep_two,
    gate_one,
    gate_two,
    up_one,
    down_one,
    up_two,
    down_two,
):
    route_one, route_two, keep_one, keep_two, gate_one, gate_two = (
        v.reshape(1, COUNT) for v in (route_one, route_two, keep_one, keep_two, gate_one, gate_two)
    )
    up_one, down_one = up_one[0], down_one[0]
    slots, tall, ints = shape(SLOTS, WIDTH), shape(COUNT, WIDTH), shape(1, COUNT, jnp.int32)

    up_mine = own_or(up_two[0], swap_pairs(up_two[0]))
    down_mine = own_or(down_two[0], swap_pairs(down_two[0]))
    up_other = other_core(up_mine)
    down_other = other_core(down_mine)

    filled_one, target_one, target_two = call(
        first_kernel, (slots, ints, ints), (route_one, keep_one, route_two, keep_two, tokens), ahead=5
    )
    rows_one = exchange_one(filled_one)
    out_one, hidden_one, slope_one = call(
        one_forward, (slots,) * 3, (rows_one, up_one, down_one), 2.2, {1: (1, 3), 2: (1, 3)},
        vmem=32, free=(0,), ahead=1,
    )
    returned_one = exchange_one(out_one)
    halves_t = shape(HALF, 2 * SLOTS)
    other_slope, hidden_t, rows_t = call(
        one_side, (slots, halves_t, halves_t), (other_y(rows_one), up_one, hidden_one, rows_one), 25,
        {1: (1, 3)}, scratch=[pltpu.VMEM((SLOTS, WIDTH), BF)] + [pltpu.VMEM((HALF, SLOTS), BF)] * 2,
        vmem=32, free=(3,),
    )

    middle, filled_two = call(
        middle_kernel, (tall, shape(SLOTS, 2 * WIDTH)),
        (target_one, target_two, gate_one, gate_two, upstream, returned_one, tokens), 0.3,
        vmem=24, free=(5,), ahead=7,
    )
    arrived = exchange_two(filled_two)
    back_two, hidden_two, inner_two = call(
        two_main, (slots,) * 3, (arrived, up_mine, down_mine, up_other, down_other), 3.3, {0: (1, 2)},
        vmem=32, free=(0,), ahead=2, after=(other_slope,),
    )
    returned_back = exchange_two(back_two)
    halves = (shape(WIDTH, HALF), shape(HALF, WIDTH))
    term_up, term_down = call(
        two_grads_other, halves, (arrived, inner_two, hidden_two), 1.2, {0: (1, 2)}, vmem=28, free=(0,),
        cost=0.02,
    )
    sum_up, sum_down = call(
        two_grads_mine, halves,
        (arrived, inner_two, hidden_two, other_core(term_up), other_core(term_down)), 1.2, {0: (1, 2)},
        vmem=32, free=(0,), cost=0.02,
    )
    moved_up, moved_down = swap_pairs(sum_up), swap_pairs(sum_down)
    grad_up_two, grad_down_two = own_or(sum_up, moved_up), own_or(sum_down, moved_down)
    (out_two,) = call(
        two_out, (slots,), (hidden_two, down_mine, down_other), 1.0, vmem=24, after=(sum_up,), cost=0.02
    )

    grad_middle, filled_back = call(
        turn_kernel, (tall, shape(2 * SLOTS, WIDTH)),
        (target_one, target_two, gate_one, returned_back, middle, upstream), 0.3,
        vmem=24, free=(3,), ahead=6, after=(sum_up, sum_down, out_two),
    )
    grads_one = exchange_pairs(filled_back)
    both, single = shape(SHARE, 2 * WIDTH), shape(SHARE, WIDTH)
    inner_one, to_next, to_last, add_next, add_last, own = call(
        one_back, (slots, both, both, single, single, both),
        (down_one, slope_one, other_slope, hidden_t, rows_t), 4.0, {0: (0, 3)},
        scratch=[
            pltpu.VMEM((2, EXPERTS_ONE, CAP_ONE, WIDTH), BF),
            pltpu.VMEM((2 * SLOTS, WIDTH), BF),
            pltpu.SemaphoreType.DMA((4,)),
        ],
        vmem=44, raw=(grads_one,), after=(echo(grads_one.reshape(-1, WIDTH)),),
    )
    returned_out = exchange_two(hold(out_two, (grads_one,)))
    (back_one,) = call(
        one_back_rows, (slots,), (inner_one, up_one), 1.0, {1: (0, 3)}, after=(moved_up, moved_down)
    )
    returned_last = exchange_one(hold(back_one, (returned_out,)))

    from_last, from_next = x_step(to_next, 1), x_step(to_last, 3)
    on_next, on_last = call(
        pass_on, (single, single), (add_next, from_last, add_last, from_next),
        after=(grad_up_two, grad_down_two), free=(1, 3),
    )
    (result,) = call(result_kernel, (tall,), (target_two, gate_two, returned_out, middle), free=(2,))
    (grad_tokens,) = call(last_kernel, (tall,), (target_one, returned_last, tokens, grad_middle), free=(1,))
    share_down, share_up = call(
        last_sums, (single, single),
        (own, from_next, from_last, x_step(on_next, 1), x_step(on_last, 3)),
        after=(result, grad_tokens), free=(3, 4),
    )
    return (
        result,
        grad_tokens,
        share_up[None],
        share_down[None],
        grad_up_two[None],
        grad_down_two[None],
    )


def solution(mesh):
    fine = Mesh(mesh.devices.reshape(2, 4, 2, 2, 4), AXES)
    rows = P(AXES, None)
    weights = P(AXES, None, None)
    return jax.shard_map(
        per_device,
        mesh=fine,
        in_specs=(
            rows, rows, rows, rows, P(AXES), P(AXES), rows, rows,
            P(EX, None, None), P(EX, None, None), weights, weights,
        ),
        out_specs=(rows, rows, P(EX, EY, None), P(EX, EY, None), weights, weights),
        check_vma=False,
    )
```

```python
import jax
import jax.numpy as jnp
from jax import lax
from jax.experimental import pallas as pl
from jax.experimental.pallas import tpu as pltpu
from jax.sharding import Mesh
from jax.sharding import PartitionSpec as P

EPS = 1e-06
AXES = ("y_hi", "z", "core", "y_lo", "x")
EX = ("y_hi", "z", "core")
EY = ("y_lo", "x")
PAIRED = ("y_hi", "z", "core", "y_lo")
CHIPS = ("y_hi", "z", "y_lo", "x")
EXPERTS_ONE, CAP_ONE = 16, 32
EXPERTS_TWO, CAP_TWO = 64, 8
WIDTH, HALF, COUNT, SLOTS = 1536, 768, 256, 512
SHARE = WIDTH // 8
BF, F32 = jnp.bfloat16, jnp.float32
CHUNK = 512
CHUNKS = [slice(start, start + CHUNK) for start in range(0, WIDTH, CHUNK)]
MIB = 1024 * 1024


def dot(left, right):
    return jnp.dot(left, right, preferred_element_type=F32)


def dot_nt(left, right):
    return lax.dot_general(left, right, (((1,), (1,)), ((), ())), preferred_element_type=F32)


def dot_tn(left, right):
    return lax.dot_general(left, right, (((0,), (0,)), ((), ())), preferred_element_type=F32)


def shape(rows, columns, dtype=BF):
    return jax.ShapeDtypeStruct((rows, columns), dtype)


def pieces_of(dims, axis, count):
    size = dims[axis] // count
    return [
        tuple(slice(i * size, (i + 1) * size) if d == axis else slice(0, dims[d]) for d in range(2))
        for i in range(count)
    ]


class Arrivals:
    def __init__(self, ahead):
        self.ahead, self.copies, self.begun, self.done = ahead, [], 0, set()

    def wait(self, number):
        while self.begun < min(number + 1 + self.ahead, len(self.copies)):
            self.copies[self.begun].start()
            self.begun += 1
        if number not in self.done:
            self.copies[number].wait()
            self.done.add(number)


class Input:
    def __init__(self, source, target, pieces, sems, arrivals):
        self.ref, self.arrivals, self.numbers = target, arrivals, []
        for piece in pieces:
            number = len(arrivals.copies)
            arrivals.copies.append(
                pltpu.make_async_copy(source.at[piece], target.at[piece], sems.at[number])
            )
            self.numbers.append(number)

    def get(self, upto=None):
        for number in self.numbers if upto is None else self.numbers[: upto + 1]:
            self.arrivals.wait(number)
        return self.ref


class Output:
    def __init__(self, source, target, sems):
        self.ref, self.target, self.sems, self.leaving = source, target, sems, []

    def send(self, rows=slice(None), columns=slice(None)):
        copy = pltpu.make_async_copy(
            self.ref.at[rows, columns], self.target.at[rows, columns], self.sems.at[len(self.leaving)]
        )
        copy.start()
        self.leaving.append(copy)

    def put(self, columns, value):
        self.ref[:, columns] = value.astype(self.ref.dtype)
        self.send(columns=columns)

    def put_all(self, value):
        self.ref[...] = value.astype(self.ref.dtype)
        self.send()


MOST_PIECES = 6


def call(kernel, outs, args, products=0.1, split=(), scratch=(), vmem=24, after=(), free=(), ahead=4,
         raw=(), cost=1.0):
    split = dict(split)
    pieces = [pieces_of(a.shape, *split.get(i, (0, 1))) for i, a in enumerate(args)]
    in_sems = sum(len(p) for p in pieces)
    inputs, results = len(args), len(outs)

    def body(*refs):
        refs = list(refs)
        sources, refs = refs[:inputs], refs[inputs:]
        own_work, refs = refs[: len(raw)], refs[len(raw) + len(after) :]
        targets, refs = refs[:results], refs[results:]
        held, refs = refs[:inputs], refs[inputs:]
        made, refs = refs[:results], refs[results:]
        arriving, leaving, extra = refs[0], refs[1], refs[2:]
        arrivals = Arrivals(ahead)
        ins = [
            Input(source, target, parts, arriving, arrivals)
            for source, target, parts in zip(sources, held, pieces)
        ]
        while arrivals.begun < min(ahead, len(arrivals.copies)):
            arrivals.copies[arrivals.begun].start()
            arrivals.begun += 1
        sends = [
            Output(source, target, leaving.at[i]) for i, (source, target) in enumerate(zip(made, targets))
        ]
        kernel(ins, sends, *own_work, *extra)
        for one in ins:
            one.get()
        for one in sends:
            for copy in one.leaving:
                copy.wait()

    moved = sum(a.size * a.dtype.itemsize for a in (*args, *outs))
    hbm = pl.BlockSpec(memory_space=pltpu.MemorySpace.HBM)
    anywhere = pl.BlockSpec(memory_space=pl.ANY)
    in_hbm = [
        a if i in free else pltpu.with_memory_space_constraint(a, pltpu.MemorySpace.HBM)
        for i, a in enumerate(args)
    ]
    return pl.pallas_call(
        body,
        out_shape=tuple(pltpu.MemorySpace.HBM(o.shape, o.dtype) for o in outs),
        in_specs=[anywhere if i in free else hbm for i in range(inputs)]
        + [hbm] * len(raw)
        + [hbm] * len(after),
        out_specs=tuple([hbm] * results),
        scratch_shapes=[pltpu.VMEM(a.shape, a.dtype) for a in args]
        + [pltpu.VMEM(o.shape, o.dtype) for o in outs]
        + [pltpu.SemaphoreType.DMA((in_sems,)), pltpu.SemaphoreType.DMA((results, MOST_PIECES))]
        + list(scratch),
        compiler_params=pltpu.CompilerParams(vmem_limit_bytes=vmem * MIB),
        cost_estimate=pl.CostEstimate(
            flops=int(cost * products * 2 * SLOTS * WIDTH * WIDTH), bytes_accessed=int(cost * moved),
            transcendentals=0,
        ),
    )(*in_hbm, *[pltpu.with_memory_space_constraint(a, pltpu.MemorySpace.HBM) for a in (*raw, *after)])


def hold(values, after):
    def nothing(*refs):
        del refs

    return pl.pallas_call(
        nothing,
        out_shape=pltpu.MemorySpace.HBM(values.shape, values.dtype),
        in_specs=[pl.BlockSpec(memory_space=pltpu.MemorySpace.HBM)]
        + [pl.BlockSpec(memory_space=pl.ANY)] * len(after),
        out_specs=pl.BlockSpec(memory_space=pltpu.MemorySpace.HBM),
        input_output_aliases={0: 0},
        compiler_params=pltpu.CompilerParams(vmem_limit_bytes=MIB),
    )(pltpu.with_memory_space_constraint(values, pltpu.MemorySpace.HBM), *after)


def iota(dims, axis):
    return lax.broadcasted_iota(jnp.int32, dims, axis)


def slot_targets(route, keep, experts, cap, index_of):
    chosen = iota((experts, COUNT), 0) == route
    earlier = (iota((COUNT, COUNT), 0) < iota((COUNT, COUNT), 1)).astype(F32).astype(BF)
    before = dot(chosen.astype(F32).astype(BF), earlier)
    rank = jnp.sum(jnp.where(chosen, before, 0.0), axis=0, keepdims=True).astype(jnp.int32)
    return jnp.where(keep > 0, index_of(route) * cap + rank, -1)


def chip_of(expert):
    return (expert // 8) * 8 + (expert % 4) * 2 + (expert // 4) % 2


def column_of(row):
    same = iota((COUNT, COUNT), 0) == iota((COUNT, COUNT), 1)
    return jnp.sum(jnp.where(same, row, jnp.zeros_like(row)), axis=1, keepdims=True)


def place_matrix(target):
    return (iota((SLOTS, COUNT), 0) == target).astype(F32).astype(BF)


def collect_matrix(target):
    column = column_of(target.astype(F32)).astype(jnp.int32)
    return (iota((COUNT, SLOTS), 1) == column).astype(F32).astype(BF)


def inverse_rms(values):
    return lax.rsqrt(jnp.mean(values * values, axis=-1, keepdims=True) + EPS)


def rms_back(values, grad):
    inv = inverse_rms(values)
    normed = values * inv
    return inv * (grad - normed * jnp.mean(grad * normed, axis=-1, keepdims=True))


def first_kernel(ins, outs):
    route1, keep1, route2, keep2, tokens = ins
    rows1, target1, target2 = outs
    to_one = slot_targets(route1.get()[...], keep1.get()[...], EXPERTS_ONE, CAP_ONE, lambda e: e)
    to_two = slot_targets(route2.get()[...], keep2.get()[...], EXPERTS_TWO, CAP_TWO, chip_of)
    target1.put_all(to_one)
    target2.put_all(to_two)
    matrix = place_matrix(to_one)
    values = tokens.get()[...].astype(F32)
    normed = (values * inverse_rms(values)).astype(BF)
    for part in CHUNKS:
        rows1.put(part, dot(matrix, normed[:, part]))


def middle_kernel(ins, outs):
    target1, target2, gate1, gate2, upstream, returned, tokens = ins
    middle, rows2 = outs
    collect = collect_matrix(target1.get()[...])
    place = place_matrix(target2.get()[...])
    gate = column_of(gate1.get()[...])
    send = (column_of(gate2.get()[...]) * upstream.get()[...].astype(F32)).astype(BF)
    for part in CHUNKS:
        rows2.put(slice(part.start + WIDTH, part.stop + WIDTH), dot(place, send[:, part]))
    gathered = dot(collect, returned.get()[...])
    mid = (tokens.get()[...].astype(F32) + gate * gathered).astype(BF)
    middle.put_all(mid)
    values = mid.astype(F32)
    normed = (values * inverse_rms(values)).astype(BF)
    for part in CHUNKS:
        rows2.put(part, dot(place, normed[:, part]))


def turn_kernel(ins, outs):
    target1, target2, gate1, returned, middle, upstream = ins
    grad_middle, rows1 = outs
    collect = collect_matrix(target2.get()[...])
    row = iota((2 * SLOTS, COUNT), 0)
    slot = row // (2 * CAP_ONE) * CAP_ONE + lax.rem(row, CAP_ONE)
    place = (slot == target1.get()[...]).astype(F32).astype(BF)
    gate = column_of(gate1.get()[...])
    gathered = dot(collect, returned.get()[...])
    grad = (
        upstream.get()[...].astype(F32) + rms_back(middle.get()[...].astype(F32), gathered)
    ).astype(BF)
    grad_middle.put_all(grad)
    send = (gate * grad.astype(F32)).astype(BF)
    for part in CHUNKS:
        rows1.put(part, dot(place, send[:, part]))


def result_kernel(ins, outs):
    target2, gate2, returned, middle = ins
    collect = collect_matrix(target2.get()[...])
    gate = column_of(gate2.get()[...])
    gathered = dot(collect, returned.get()[...])
    outs[0].put_all(middle.get()[...].astype(F32) + gate * gathered)


def last_kernel(ins, outs):
    target1, returned, tokens, grad_middle = ins
    collect = collect_matrix(target1.get()[...])
    gathered = dot(collect, returned.get()[...])
    outs[0].put_all(
        grad_middle.get()[...].astype(F32) + rms_back(tokens.get()[...].astype(F32), gathered)
    )


def one_forward(ins, outs):
    rows, up, down = ins
    out, hidden, slope = outs
    rows = rows.get()
    for number, part in enumerate(CHUNKS):
        pre = dot(rows[...], up.get(number)[:, part])
        sigma = jax.nn.sigmoid(pre)
        hidden.put(part, pre * sigma)
        slope.put(part, sigma * (1.0 + pre * (1.0 - sigma)))
    for number, part in enumerate(CHUNKS):
        out.put(part, dot(hidden.ref[...], down.get(number)[:, part]))


def one_side(ins, outs, hidden_v, own_rows, own_hidden):
    rows, up, first_hidden, first_rows = ins
    slope, hidden_t, rows_t = outs
    y_lo, x = lax.axis_index("y_lo"), lax.axis_index("x")
    rows = rows.get()
    for number, part in enumerate(CHUNKS):
        pre = dot(rows[...], up.get(number)[:, part])
        sigma = jax.nn.sigmoid(pre)
        hidden_v[:, part] = (pre * sigma).astype(BF)
        slope.put(part, sigma * (1.0 + pre * (1.0 - sigma)))
    same = (iota((SLOTS, SLOTS), 0) == iota((SLOTS, SLOTS), 1)).astype(F32).astype(BF)
    columns = pl.ds(pl.multiple_of(y_lo * HALF, HALF), HALF)
    for sources, target, wide in (
        ((first_hidden.get(), hidden_v), hidden_t, own_hidden),
        ((first_rows.get(), rows), rows_t, own_rows),
    ):
        for number, source in enumerate(sources):
            wide[...] = dot_tn(source[:, columns], same).astype(BF)
            for k in range(4):
                begin = pl.multiple_of(lax.rem(x + k, 4) * SHARE, SHARE)
                target.ref[k * SHARE : (k + 1) * SHARE, number * SLOTS : (number + 1) * SLOTS] = (
                    wide[pl.ds(begin, SHARE), :]
                )
        target.send()


def bring_grads(grads, grads_v, sems):
    number = lax.rem(lax.axis_index("y_hi") + lax.axis_index("y_lo"), 2)
    half = EXPERTS_ONE // 2
    copies = [
        pltpu.make_async_copy(
            grads.at[y_hi * half : (y_hi + 1) * half, lax.rem(number + y_hi + j, 2)],
            grads_v.at[j, y_hi * half : (y_hi + 1) * half],
            sems.at[2 * j + y_hi],
        )
        for j in range(2)
        for y_hi in range(2)
    ]
    for copy in copies:
        copy.start()

    def wait(j):
        copies[2 * j].wait()
        copies[2 * j + 1].wait()

    return wait


def put_shares(left, right, targets):
    for part in CHUNKS:
        product = dot(left[...], right(part)).astype(BF)
        for k, target in enumerate(targets):
            target.put(part, product[k * SHARE : (k + 1) * SHARE])


def one_back_down(ins, outs, grads, grads_v, sems):
    wait = bring_grads(grads, grads_v, sems)
    left = ins[0].get()
    wait(0)
    wait(1)
    put_shares(left, lambda part: grads_v[:, :, :, part].reshape(2 * SLOTS, CHUNK), outs)


def one_back_up(ins, outs, grads, grads_v, inner_v, sems):
    down, slope, other_slope, rows_t, up = ins
    wait = bring_grads(grads, grads_v, sems)
    down.get(0)
    for j, factor in enumerate((slope, other_slope)):
        wait(j)
        here = slice(j * SLOTS, (j + 1) * SLOTS)
        for number, part in enumerate(CHUNKS):
            back = dot_nt(grads_v[j].reshape(SLOTS, WIDTH), down.get(number)[part, :])
            inner_v[here, part] = (back * factor.get()[:, part].astype(F32)).astype(BF)
    put_shares(rows_t.get(), lambda part: inner_v[:, part], outs[1:])
    for number, part in enumerate(CHUNKS):
        outs[0].put(part, dot_nt(inner_v[:SLOTS, :], up.get(number)[part, :]))


def two_main(ins, outs):
    arrived, up_mine, down_mine, up_other, down_other = ins
    back, mine, other = outs
    for target, up, down in ((mine, up_mine, down_mine), (other, up_other, down_other)):
        pre = dot(arrived.get(0)[:, :WIDTH], up.get()[...])
        sigma = jax.nn.sigmoid(pre)
        grad = dot_nt(arrived.get()[:, WIDTH:], down.get()[...])
        target.put(slice(HALF, WIDTH), pre * sigma)
        target.put(slice(0, HALF), grad * (sigma * (1.0 + pre * (1.0 - sigma))))
    for part in CHUNKS:
        back.put(
            part,
            dot_nt(mine.ref[:, :HALF], up_mine.ref[part, :])
            + dot_nt(other.ref[:, :HALF], up_other.ref[part, :]),
        )


def two_grads(ins, outs):
    arrived, mine, arrived_there, got = ins
    here, there = arrived.get()[:, :WIDTH], mine.get()[:, :HALF]
    up = dot_tn(here, there) + dot_tn(arrived_there.get()[:, :WIDTH], got.get()[:, :HALF])
    outs[0].put(slice(0, HALF), up)
    down = dot_tn(mine.ref[:, HALF:], arrived.ref[:, WIDTH:])
    down = (down + dot_tn(got.ref[:, HALF:], arrived_there.ref[:, WIDTH:])).astype(BF)
    for number in range(2):
        rows = slice(number * HALF, (number + 1) * HALF)
        outs[0].ref[rows, HALF:] = down[:, rows]
    outs[0].send(columns=slice(HALF, WIDTH))


def two_out(ins, outs):
    mine, other, down_mine, down_other = ins
    mine, other = mine.get(), other.get()
    for part in CHUNKS:
        outs[0].put(
            part,
            dot(mine[:, HALF:], down_mine.get()[:, part])
            + dot(other[:, HALF:], down_other.get()[:, part]),
        )


def total(*parts):
    result = parts[0].astype(F32)
    for part in parts[1:]:
        result = result + part.astype(F32)
    return result


def pass_on(ins, outs):
    outs[0].put_all(total(ins[0].get()[...], ins[1].get()[...]))


def last_sums(ins, outs):
    for number, target in enumerate(outs):
        target.put_all(total(*[one.get()[...] for one in ins[3 * number : 3 * number + 3]]))


NEAREST = [
    [
        ((y_hi * 4 + z) * 2 + core) * 2 + (number ^ y_hi)
        for y_hi in range(2)
        for z in range(4)
        for core in range(2)
    ]
    for number in range(2)
]


def exchange_one(rows):
    parts = rows.reshape(EXPERTS_ONE, CAP_ONE, rows.shape[1])
    return lax.all_to_all(
        parts, PAIRED, split_axis=0, concat_axis=0, tiled=True, axis_index_groups=NEAREST
    ).reshape(rows.shape)


def exchange_pairs(rows):
    parts = rows.reshape(2 * EXPERTS_ONE, CAP_ONE, WIDTH)
    parts = lax.all_to_all(parts, PAIRED, split_axis=0, concat_axis=0, tiled=True)
    return parts.reshape(EXPERTS_ONE, 2, CAP_ONE, WIDTH)


def exchange_two(rows):
    parts = rows.reshape(EXPERTS_TWO, CAP_TWO, rows.shape[1])
    return lax.all_to_all(parts, CHIPS, split_axis=0, concat_axis=0, tiled=True).reshape(rows.shape)


def swap_pairs(values):
    size = 4
    pairs = []
    for x in range(0, size, 2):
        pairs += [(size + x, x + 1), (x + 1, size + x)]
    return lax.ppermute(values, ("core", "x"), pairs)


def own_or(values, moved):
    stays = lax.axis_index("core") == lax.axis_index("x") % 2
    return jnp.where(stays, values, moved)


def other_core(values):
    return lax.ppermute(values, "core", [(0, 1), (1, 0)])


def other_y(values):
    return lax.ppermute(values, "y_lo", [(0, 1), (1, 0)])


def x_step(values, by):
    return lax.ppermute(values, "x", [(i, (i + by) % 4) for i in range(4)])


def per_device(
    tokens,
    upstream,
    route_one,
    route_two,
    keep_one,
    keep_two,
    gate_one,
    gate_two,
    up_one,
    down_one,
    up_two,
    down_two,
):
    route_one, route_two, keep_one, keep_two, gate_one, gate_two = (
        v.reshape(1, COUNT) for v in (route_one, route_two, keep_one, keep_two, gate_one, gate_two)
    )
    up_one, down_one = up_one[0], down_one[0]
    slots, tall, ints = shape(SLOTS, WIDTH), shape(COUNT, WIDTH), shape(1, COUNT, jnp.int32)

    up_mine = own_or(up_two[0], swap_pairs(up_two[0]))
    down_mine = own_or(down_two[0], swap_pairs(down_two[0]))
    up_other = other_core(up_mine)
    down_other = other_core(down_mine)

    filled_one, target_one, target_two = call(
        first_kernel, (slots, ints, ints), (route_one, keep_one, route_two, keep_two, tokens), ahead=5
    )
    rows_one = exchange_one(filled_one)
    out_one, hidden_one, slope_one = call(
        one_forward, (slots,) * 3, (rows_one, up_one, down_one), 2.2, {1: (1, 3), 2: (1, 3)},
        vmem=32, free=(0,), ahead=1,
    )
    returned_one = exchange_one(out_one)
    halves_t = shape(HALF, 2 * SLOTS)
    rows_there = other_y(rows_one)
    other_slope, hidden_t, rows_t = call(
        one_side, (slots, halves_t, halves_t), (rows_there, up_one, hidden_one, rows_one), 12,
        {1: (1, 3)}, scratch=[pltpu.VMEM((SLOTS, WIDTH), BF)] + [pltpu.VMEM((HALF, SLOTS), BF)] * 2,
        vmem=32, free=(3,),
    )

    middle, filled_two = call(
        middle_kernel, (tall, shape(SLOTS, 2 * WIDTH)),
        (target_one, target_two, gate_one, gate_two, upstream, returned_one, tokens), 0.3,
        vmem=24, free=(5,), ahead=7, after=(up_mine, rows_there),
    )
    arrived = exchange_two(filled_two)
    back_two, mine_two, other_two = call(
        two_main, (slots,) * 3, (arrived, up_mine, down_mine, up_other, down_other), 3.3, {0: (1, 2)},
        vmem=32, free=(0,), ahead=2,
    )
    returned_back = exchange_two(back_two)
    (sums_two,) = call(
        two_grads, (shape(WIDTH, WIDTH),),
        (arrived, mine_two, other_core(arrived), other_core(other_two)), 2.2, vmem=36, free=(0, 2), cost=0.02,
    )
    moved_two = swap_pairs(sums_two)
    grads_two = own_or(sums_two, moved_two)
    grad_up_two = grads_two[:, :HALF]
    grad_down_two = jnp.concatenate([grads_two[:HALF, HALF:], grads_two[HALF:, HALF:]], 1)
    grad_middle, filled_back = call(
        turn_kernel, (tall, shape(2 * SLOTS, WIDTH)),
        (target_one, target_two, gate_one, returned_back, middle, upstream), 0.3,
        vmem=24, free=(3,), ahead=6, after=(sums_two,),
    )
    (out_two,) = call(
        two_out, (slots,), (mine_two, other_two, down_mine, down_other), 1.0, vmem=24, cost=0.02,
        after=(filled_back, other_slope),
    )
    grads_one = exchange_pairs(filled_back)
    here = grads_one[0, 0, :16, :128]
    single = shape(SHARE, WIDTH)
    held = pltpu.VMEM((2, EXPERTS_ONE, CAP_ONE, WIDTH), BF)
    own_down, add_down, far_down, near_down = call(
        one_back_down, (single,) * 4, (hidden_t,), 1.2, scratch=[held, pltpu.SemaphoreType.DMA((4,))],
        vmem=32, raw=(grads_one,), after=(other_core(here),),
    )
    back_one, own_up, near_up, far_up, add_up = call(
        one_back_up, (slots, *[single] * 4), (down_one, slope_one, other_slope, rows_t, up_one), 4.2,
        {0: (0, 3), 4: (0, 3)},
        scratch=[held, pltpu.VMEM((2 * SLOTS, WIDTH), BF), pltpu.SemaphoreType.DMA((4,))],
        vmem=48, raw=(grads_one,), after=(far_down,),
    )
    returned_out = exchange_two(hold(out_two, (here,)))
    returned_last = exchange_one(hold(back_one, (returned_out,)))

    (on_down,) = call(pass_on, (single,), (add_down, x_step(far_down, 1)), free=(1,), after=(moved_two,))
    from_next = x_step(near_down, 3)
    from_last = x_step(near_up, 1)
    (on_up,) = call(
        pass_on, (single,), (add_up, x_step(far_up, 3)), free=(1,), after=(grad_up_two, grad_down_two)
    )
    (result,) = call(result_kernel, (tall,), (target_two, gate_two, returned_out, middle), free=(2,))
    (grad_tokens,) = call(last_kernel, (tall,), (target_one, returned_last, tokens, grad_middle), free=(1,))
    share_down, share_up = call(
        last_sums, (single, single),
        (own_down, from_next, x_step(on_down, 1), own_up, from_last, x_step(on_up, 3)),
        free=(1, 2, 4, 5), after=(result, grad_tokens), ahead=6,
    )
    return (
        result,
        grad_tokens,
        share_up[None],
        share_down[None],
        grad_up_two[None],
        grad_down_two[None],
    )


def solution(mesh):
    fine = Mesh(mesh.devices.reshape(2, 4, 2, 2, 4), AXES)
    rows = P(AXES, None)
    weights = P(AXES, None, None)
    return jax.shard_map(
        per_device,
        mesh=fine,
        in_specs=(
            rows, rows, rows, rows, P(AXES), P(AXES), rows, rows,
            P(EX, None, None), P(EX, None, None), weights, weights,
        ),
        out_specs=(rows, rows, P(EX, EY, None), P(EX, EY, None), weights, weights),
        check_vma=False,
    )
```

```python
import jax
import jax.numpy as jnp
from jax import lax
from jax.experimental import pallas as pl
from jax.experimental.pallas import tpu as pltpu
from jax.sharding import Mesh
from jax.sharding import PartitionSpec as P

EPS = 1e-06
AXES = ("y_hi", "z", "core", "y_lo", "x")
EX = ("y_hi", "z", "core")
EY = ("y_lo", "x")
PAIRED = ("y_hi", "z", "core", "y_lo")
CHIPS = ("y_hi", "z", "y_lo", "x")
EXPERTS_ONE, CAP_ONE = 16, 32
EXPERTS_TWO, CAP_TWO = 64, 8
WIDTH, HALF, COUNT, SLOTS = 1536, 768, 256, 512
SHARE = WIDTH // 8
BF, F32 = jnp.bfloat16, jnp.float32
CHUNK = 512
CHUNKS = [slice(start, start + CHUNK) for start in range(0, WIDTH, CHUNK)]
MIB = 1024 * 1024


def dot(left, right):
    return jnp.dot(left, right, preferred_element_type=F32)


def dot_nt(left, right):
    return lax.dot_general(left, right, (((1,), (1,)), ((), ())), preferred_element_type=F32)


def dot_tn(left, right):
    return lax.dot_general(left, right, (((0,), (0,)), ((), ())), preferred_element_type=F32)


def shape(rows, columns, dtype=BF):
    return jax.ShapeDtypeStruct((rows, columns), dtype)


def pieces_of(dims, axis, count):
    size = dims[axis] // count
    return [
        tuple(slice(i * size, (i + 1) * size) if d == axis else slice(0, dims[d]) for d in range(2))
        for i in range(count)
    ]


class Arrivals:
    def __init__(self, ahead):
        self.ahead, self.copies, self.begun, self.done = ahead, [], 0, set()

    def wait(self, number):
        while self.begun < min(number + 1 + self.ahead, len(self.copies)):
            self.copies[self.begun].start()
            self.begun += 1
        if number not in self.done:
            self.copies[number].wait()
            self.done.add(number)


class Input:
    def __init__(self, source, target, pieces, sems, arrivals):
        self.ref, self.arrivals, self.numbers = target, arrivals, []
        for piece in pieces:
            number = len(arrivals.copies)
            arrivals.copies.append(
                pltpu.make_async_copy(source.at[piece], target.at[piece], sems.at[number])
            )
            self.numbers.append(number)

    def get(self, upto=None):
        for number in self.numbers if upto is None else self.numbers[: upto + 1]:
            self.arrivals.wait(number)
        return self.ref


class Output:
    def __init__(self, source, target, sems):
        self.ref, self.target, self.sems, self.leaving = source, target, sems, []

    def send(self, rows=slice(None), columns=slice(None)):
        copy = pltpu.make_async_copy(
            self.ref.at[rows, columns], self.target.at[rows, columns], self.sems.at[len(self.leaving)]
        )
        copy.start()
        self.leaving.append(copy)

    def put(self, columns, value):
        self.ref[:, columns] = value.astype(self.ref.dtype)
        self.send(columns=columns)

    def put_all(self, value):
        self.ref[...] = value.astype(self.ref.dtype)
        self.send()


MOST_PIECES = 6


def call(kernel, outs, args, products=0.1, split=(), scratch=(), vmem=24, after=(), free=(), ahead=4,
         raw=(), cost=1.0):
    split = dict(split)
    pieces = [pieces_of(a.shape, *split.get(i, (0, 1))) for i, a in enumerate(args)]
    in_sems = sum(len(p) for p in pieces)
    inputs, results = len(args), len(outs)

    def body(*refs):
        refs = list(refs)
        sources, refs = refs[:inputs], refs[inputs:]
        own_work, refs = refs[: len(raw)], refs[len(raw) + len(after) :]
        targets, refs = refs[:results], refs[results:]
        held, refs = refs[:inputs], refs[inputs:]
        made, refs = refs[:results], refs[results:]
        arriving, leaving, extra = refs[0], refs[1], refs[2:]
        arrivals = Arrivals(ahead)
        ins = [
            Input(source, target, parts, arriving, arrivals)
            for source, target, parts in zip(sources, held, pieces)
        ]
        while arrivals.begun < min(ahead, len(arrivals.copies)):
            arrivals.copies[arrivals.begun].start()
            arrivals.begun += 1
        sends = [
            Output(source, target, leaving.at[i]) for i, (source, target) in enumerate(zip(made, targets))
        ]
        kernel(ins, sends, *own_work, *extra)
        for one in ins:
            one.get()
        for one in sends:
            for copy in one.leaving:
                copy.wait()

    moved = sum(a.size * a.dtype.itemsize for a in (*args, *outs))
    hbm = pl.BlockSpec(memory_space=pltpu.MemorySpace.HBM)
    anywhere = pl.BlockSpec(memory_space=pl.ANY)
    in_hbm = [
        a if i in free else pltpu.with_memory_space_constraint(a, pltpu.MemorySpace.HBM)
        for i, a in enumerate(args)
    ]
    return pl.pallas_call(
        body,
        out_shape=tuple(pltpu.MemorySpace.HBM(o.shape, o.dtype) for o in outs),
        in_specs=[anywhere if i in free else hbm for i in range(inputs)]
        + [hbm] * len(raw)
        + [hbm] * len(after),
        out_specs=tuple([hbm] * results),
        scratch_shapes=[pltpu.VMEM(a.shape, a.dtype) for a in args]
        + [pltpu.VMEM(o.shape, o.dtype) for o in outs]
        + [pltpu.SemaphoreType.DMA((in_sems,)), pltpu.SemaphoreType.DMA((results, MOST_PIECES))]
        + list(scratch),
        compiler_params=pltpu.CompilerParams(vmem_limit_bytes=vmem * MIB),
        cost_estimate=pl.CostEstimate(
            flops=int(cost * products * 2 * SLOTS * WIDTH * WIDTH), bytes_accessed=int(cost * moved),
            transcendentals=0,
        ),
    )(*in_hbm, *[pltpu.with_memory_space_constraint(a, pltpu.MemorySpace.HBM) for a in (*raw, *after)])


def hold(values, after):
    def nothing(*refs):
        del refs

    return pl.pallas_call(
        nothing,
        out_shape=pltpu.MemorySpace.HBM(values.shape, values.dtype),
        in_specs=[pl.BlockSpec(memory_space=pltpu.MemorySpace.HBM)]
        + [pl.BlockSpec(memory_space=pl.ANY)] * len(after),
        out_specs=pl.BlockSpec(memory_space=pltpu.MemorySpace.HBM),
        input_output_aliases={0: 0},
        compiler_params=pltpu.CompilerParams(vmem_limit_bytes=MIB),
    )(pltpu.with_memory_space_constraint(values, pltpu.MemorySpace.HBM), *after)


def iota(dims, axis):
    return lax.broadcasted_iota(jnp.int32, dims, axis)


def slot_targets(route, keep, experts, cap, index_of):
    chosen = iota((experts, COUNT), 0) == route
    earlier = (iota((COUNT, COUNT), 0) < iota((COUNT, COUNT), 1)).astype(F32).astype(BF)
    before = dot(chosen.astype(F32).astype(BF), earlier)
    rank = jnp.sum(jnp.where(chosen, before, 0.0), axis=0, keepdims=True).astype(jnp.int32)
    return jnp.where(keep > 0, index_of(route) * cap + rank, -1)


def chip_of(expert):
    return (expert // 8) * 8 + (expert % 4) * 2 + (expert // 4) % 2


def column_of(row):
    same = iota((COUNT, COUNT), 0) == iota((COUNT, COUNT), 1)
    return jnp.sum(jnp.where(same, row, jnp.zeros_like(row)), axis=1, keepdims=True)


def place_matrix(target):
    return (iota((SLOTS, COUNT), 0) == target).astype(F32).astype(BF)


def collect_matrix(target):
    column = column_of(target.astype(F32)).astype(jnp.int32)
    return (iota((COUNT, SLOTS), 1) == column).astype(F32).astype(BF)


def inverse_rms(values):
    return lax.rsqrt(jnp.mean(values * values, axis=-1, keepdims=True) + EPS)


def rms_back(values, grad):
    inv = inverse_rms(values)
    normed = values * inv
    return inv * (grad - normed * jnp.mean(grad * normed, axis=-1, keepdims=True))


def first_kernel(ins, outs):
    route1, keep1, route2, keep2, tokens = ins
    rows1, target1, target2 = outs
    to_one = slot_targets(route1.get()[...], keep1.get()[...], EXPERTS_ONE, CAP_ONE, lambda e: e)
    to_two = slot_targets(route2.get()[...], keep2.get()[...], EXPERTS_TWO, CAP_TWO, chip_of)
    target1.put_all(to_one)
    target2.put_all(to_two)
    matrix = place_matrix(to_one)
    values = tokens.get()[...].astype(F32)
    normed = (values * inverse_rms(values)).astype(BF)
    for part in CHUNKS:
        rows1.put(part, dot(matrix, normed[:, part]))


def middle_kernel(ins, outs):
    target1, target2, gate1, gate2, upstream, returned, tokens = ins
    middle, rows2 = outs
    collect = collect_matrix(target1.get()[...])
    place = place_matrix(target2.get()[...])
    gate = column_of(gate1.get()[...])
    send = (column_of(gate2.get()[...]) * upstream.get()[...].astype(F32)).astype(BF)
    for part in CHUNKS:
        rows2.put(slice(part.start + WIDTH, part.stop + WIDTH), dot(place, send[:, part]))
    gathered = dot(collect, returned.get()[...])
    mid = (tokens.get()[...].astype(F32) + gate * gathered).astype(BF)
    middle.put_all(mid)
    values = mid.astype(F32)
    normed = (values * inverse_rms(values)).astype(BF)
    for part in CHUNKS:
        rows2.put(part, dot(place, normed[:, part]))


def turn_kernel(ins, outs):
    target1, target2, gate1, returned, middle, upstream = ins
    grad_middle, rows1 = outs
    collect = collect_matrix(target2.get()[...])
    row = iota((2 * SLOTS, COUNT), 0)
    slot = row // (2 * CAP_ONE) * CAP_ONE + lax.rem(row, CAP_ONE)
    place = (slot == target1.get()[...]).astype(F32).astype(BF)
    gate = column_of(gate1.get()[...])
    gathered = dot(collect, returned.get()[...])
    grad = (
        upstream.get()[...].astype(F32) + rms_back(middle.get()[...].astype(F32), gathered)
    ).astype(BF)
    grad_middle.put_all(grad)
    send = (gate * grad.astype(F32)).astype(BF)
    for part in CHUNKS:
        rows1.put(part, dot(place, send[:, part]))


def result_kernel(ins, outs):
    target2, gate2, returned, middle = ins
    collect = collect_matrix(target2.get()[...])
    gate = column_of(gate2.get()[...])
    gathered = dot(collect, returned.get()[...])
    outs[0].put_all(middle.get()[...].astype(F32) + gate * gathered)


def last_kernel(ins, outs):
    target1, returned, tokens, grad_middle = ins
    collect = collect_matrix(target1.get()[...])
    gathered = dot(collect, returned.get()[...])
    outs[0].put_all(
        grad_middle.get()[...].astype(F32) + rms_back(tokens.get()[...].astype(F32), gathered)
    )


def one_forward(ins, outs):
    rows, up, down = ins
    out, hidden, slope = outs
    rows = rows.get()
    for number, part in enumerate(CHUNKS):
        pre = dot(rows[...], up.get(number)[:, part])
        sigma = jax.nn.sigmoid(pre)
        hidden.put(part, pre * sigma)
        slope.put(part, sigma * (1.0 + pre * (1.0 - sigma)))
    for number, part in enumerate(CHUNKS):
        out.put(part, dot(hidden.ref[...], down.get(number)[:, part]))


def one_side(ins, outs, hidden_v, own_rows, own_hidden):
    rows, up, first_hidden, first_rows = ins
    slope, hidden_t, rows_t = outs
    y_lo, x = lax.axis_index("y_lo"), lax.axis_index("x")
    rows = rows.get()
    for number, part in enumerate(CHUNKS):
        pre = dot(rows[...], up.get(number)[:, part])
        sigma = jax.nn.sigmoid(pre)
        hidden_v[:, part] = (pre * sigma).astype(BF)
        slope.put(part, sigma * (1.0 + pre * (1.0 - sigma)))
    same = (iota((SLOTS, SLOTS), 0) == iota((SLOTS, SLOTS), 1)).astype(F32).astype(BF)
    columns = pl.ds(pl.multiple_of(y_lo * HALF, HALF), HALF)
    for sources, target, wide in (
        ((first_hidden.get(), hidden_v), hidden_t, own_hidden),
        ((first_rows.get(), rows), rows_t, own_rows),
    ):
        for number, source in enumerate(sources):
            wide[...] = dot_tn(source[:, columns], same).astype(BF)
            for k in range(4):
                begin = pl.multiple_of(lax.rem(x + k, 4) * SHARE, SHARE)
                target.ref[k * SHARE : (k + 1) * SHARE, number * SLOTS : (number + 1) * SLOTS] = (
                    wide[pl.ds(begin, SHARE), :]
                )
        target.send()


def bring_grads(grads, grads_v, sems):
    number = lax.rem(lax.axis_index("y_hi") + lax.axis_index("y_lo"), 2)
    half = EXPERTS_ONE // 2
    copies = [
        pltpu.make_async_copy(
            grads.at[y_hi * half : (y_hi + 1) * half, lax.rem(number + y_hi + j, 2)],
            grads_v.at[j, y_hi * half : (y_hi + 1) * half],
            sems.at[2 * j + y_hi],
        )
        for j in range(2)
        for y_hi in range(2)
    ]
    for copy in copies:
        copy.start()

    def wait(j):
        copies[2 * j].wait()
        copies[2 * j + 1].wait()

    return wait


def put_shares(left, right, targets):
    for part in CHUNKS:
        product = dot(left[...], right(part)).astype(BF)
        for k, target in enumerate(targets):
            target.put(part, product[k * SHARE : (k + 1) * SHARE])


def one_back_down(ins, outs, grads, grads_v, sems):
    wait = bring_grads(grads, grads_v, sems)
    left = ins[0].get()
    wait(0)
    wait(1)
    put_shares(left, lambda part: grads_v[:, :, :, part].reshape(2 * SLOTS, CHUNK), outs)


def one_back_up(ins, outs, grads, grads_v, inner_v, sems):
    down, slope, other_slope, rows_t, up = ins
    wait = bring_grads(grads, grads_v, sems)
    down.get(0)
    for j, factor in enumerate((slope, other_slope)):
        wait(j)
        here = slice(j * SLOTS, (j + 1) * SLOTS)
        for number, part in enumerate(CHUNKS):
            back = dot_nt(grads_v[j].reshape(SLOTS, WIDTH), down.get(number)[part, :])
            inner_v[here, part] = (back * factor.get()[:, part].astype(F32)).astype(BF)
    put_shares(rows_t.get(), lambda part: inner_v[:, part], outs[1:])
    for number, part in enumerate(CHUNKS):
        outs[0].put(part, dot_nt(inner_v[:SLOTS, :], up.get(number)[part, :]))


def two_main(ins, outs):
    arrived, up_mine, down_mine, up_other, down_other = ins
    back, mine, other = outs
    for target, up, down in ((mine, up_mine, down_mine), (other, up_other, down_other)):
        pre = dot(arrived.get(0)[:, :WIDTH], up.get()[...])
        sigma = jax.nn.sigmoid(pre)
        grad = dot_nt(arrived.get()[:, WIDTH:], down.get()[...])
        target.put(slice(HALF, WIDTH), pre * sigma)
        target.put(slice(0, HALF), grad * (sigma * (1.0 + pre * (1.0 - sigma))))
    for part in CHUNKS:
        back.put(
            part,
            dot_nt(mine.ref[:, :HALF], up_mine.ref[part, :])
            + dot_nt(other.ref[:, :HALF], up_other.ref[part, :]),
        )


def two_grads(ins, outs):
    arrived, mine, arrived_there, got = ins
    here, there = arrived.get()[:, :WIDTH], mine.get()[:, :HALF]
    up = dot_tn(here, there) + dot_tn(arrived_there.get()[:, :WIDTH], got.get()[:, :HALF])
    outs[0].put(slice(0, HALF), up)
    down = dot_tn(mine.ref[:, HALF:], arrived.ref[:, WIDTH:])
    down = (down + dot_tn(got.ref[:, HALF:], arrived_there.ref[:, WIDTH:])).astype(BF)
    for number in range(2):
        rows = slice(number * HALF, (number + 1) * HALF)
        outs[0].ref[rows, HALF:] = down[:, rows]
    outs[0].send(columns=slice(HALF, WIDTH))


def two_out(ins, outs):
    mine, other, down_mine, down_other = ins
    mine, other = mine.get(), other.get()
    for part in CHUNKS:
        outs[0].put(
            part,
            dot(mine[:, HALF:], down_mine.get()[:, part])
            + dot(other[:, HALF:], down_other.get()[:, part]),
        )


def total(*parts):
    result = parts[0].astype(F32)
    for part in parts[1:]:
        result = result + part.astype(F32)
    return result


def pass_on(ins, outs):
    outs[0].put_all(total(ins[0].get()[...], ins[1].get()[...]))


def last_sums(ins, outs):
    for number, target in enumerate(outs):
        target.put_all(total(*[one.get()[...] for one in ins[3 * number : 3 * number + 3]]))


NEAREST = [
    [
        ((y_hi * 4 + z) * 2 + core) * 2 + (number ^ y_hi)
        for y_hi in range(2)
        for z in range(4)
        for core in range(2)
    ]
    for number in range(2)
]


def exchange_one(rows):
    parts = rows.reshape(EXPERTS_ONE, CAP_ONE, rows.shape[1])
    return lax.all_to_all(
        parts, PAIRED, split_axis=0, concat_axis=0, tiled=True, axis_index_groups=NEAREST
    ).reshape(rows.shape)


def exchange_pairs(rows):
    parts = rows.reshape(2 * EXPERTS_ONE, CAP_ONE, WIDTH)
    parts = lax.all_to_all(parts, PAIRED, split_axis=0, concat_axis=0, tiled=True)
    return parts.reshape(EXPERTS_ONE, 2, CAP_ONE, WIDTH)


def exchange_two(rows):
    parts = rows.reshape(EXPERTS_TWO, CAP_TWO, rows.shape[1])
    return lax.all_to_all(parts, CHIPS, split_axis=0, concat_axis=0, tiled=True).reshape(rows.shape)


def swap_pairs(values):
    size = 4
    pairs = []
    for x in range(0, size, 2):
        pairs += [(size + x, x + 1), (x + 1, size + x)]
    return lax.ppermute(values, ("core", "x"), pairs)


def own_or(values, moved):
    stays = lax.axis_index("core") == lax.axis_index("x") % 2
    return jnp.where(stays, values, moved)


def other_core(values):
    return lax.ppermute(values, "core", [(0, 1), (1, 0)])


def other_y(values):
    return lax.ppermute(values, "y_lo", [(0, 1), (1, 0)])


def x_step(values, by):
    return lax.ppermute(values, "x", [(i, (i + by) % 4) for i in range(4)])


def per_device(
    tokens,
    upstream,
    route_one,
    route_two,
    keep_one,
    keep_two,
    gate_one,
    gate_two,
    up_one,
    down_one,
    up_two,
    down_two,
):
    route_one, route_two, keep_one, keep_two, gate_one, gate_two = (
        v.reshape(1, COUNT) for v in (route_one, route_two, keep_one, keep_two, gate_one, gate_two)
    )
    up_one, down_one = up_one[0], down_one[0]
    slots, tall, ints = shape(SLOTS, WIDTH), shape(COUNT, WIDTH), shape(1, COUNT, jnp.int32)

    up_mine = own_or(up_two[0], swap_pairs(up_two[0]))
    down_mine = own_or(down_two[0], swap_pairs(down_two[0]))
    up_other = other_core(up_mine)
    down_other = other_core(down_mine)

    filled_one, target_one, target_two = call(
        first_kernel, (slots, ints, ints), (route_one, keep_one, route_two, keep_two, tokens), ahead=5
    )
    rows_one = exchange_one(filled_one)
    out_one, hidden_one, slope_one = call(
        one_forward, (slots,) * 3, (rows_one, up_one, down_one), 2.2, {1: (1, 3), 2: (1, 3)},
        vmem=32, free=(0,), ahead=1,
    )
    returned_one = exchange_one(out_one)
    halves_t = shape(HALF, 2 * SLOTS)
    rows_there = other_y(rows_one)
    other_slope, hidden_t, rows_t = call(
        one_side, (slots, halves_t, halves_t), (rows_there, up_one, hidden_one, rows_one), 12,
        {1: (1, 3)}, scratch=[pltpu.VMEM((SLOTS, WIDTH), BF)] + [pltpu.VMEM((HALF, SLOTS), BF)] * 2,
        vmem=32, free=(3,),
    )

    middle, filled_two = call(
        middle_kernel, (tall, shape(SLOTS, 2 * WIDTH)),
        (target_one, target_two, gate_one, gate_two, upstream, returned_one, tokens), 0.3,
        vmem=24, free=(5,), ahead=7, after=(up_mine, rows_there),
    )
    arrived = exchange_two(filled_two)
    back_two, mine_two, other_two = call(
        two_main, (slots,) * 3, (arrived, up_mine, down_mine, up_other, down_other), 3.3, {0: (1, 2)},
        vmem=32, free=(0,), ahead=2,
    )
    returned_back = exchange_two(back_two)
    (sums_two,) = call(
        two_grads, (shape(WIDTH, WIDTH),),
        (arrived, mine_two, other_core(arrived), other_core(other_two)), 2.2, vmem=36, free=(0, 2), cost=0.02,
    )
    moved_two = swap_pairs(sums_two)
    grads_two = own_or(sums_two, moved_two)
    grad_up_two = grads_two[:, :HALF]
    grad_down_two = jnp.concatenate([grads_two[:HALF, HALF:], grads_two[HALF:, HALF:]], 1)
    grad_middle, filled_back = call(
        turn_kernel, (tall, shape(2 * SLOTS, WIDTH)),
        (target_one, target_two, gate_one, returned_back, middle, upstream), 0.3,
        vmem=24, free=(3,), ahead=6, after=(sums_two,),
    )
    (out_two,) = call(
        two_out, (slots,), (mine_two, other_two, down_mine, down_other), 1.0, vmem=24, cost=0.02,
        after=(filled_back, other_slope),
    )
    grads_one = exchange_pairs(filled_back)
    here = grads_one[0, 0, :16, :128]
    single = shape(SHARE, WIDTH)
    held = pltpu.VMEM((2, EXPERTS_ONE, CAP_ONE, WIDTH), BF)
    own_down, add_down, far_down, near_down = call(
        one_back_down, (single,) * 4, (hidden_t,), 1.2, scratch=[held, pltpu.SemaphoreType.DMA((4,))],
        vmem=32, raw=(grads_one,), after=(other_core(here),),
    )
    back_one, own_up, near_up, far_up, add_up = call(
        one_back_up, (slots, *[single] * 4), (down_one, slope_one, other_slope, rows_t, up_one), 4.2,
        {0: (0, 3), 4: (0, 3)},
        scratch=[held, pltpu.VMEM((2 * SLOTS, WIDTH), BF), pltpu.SemaphoreType.DMA((4,))],
        vmem=48, raw=(grads_one,), after=(far_down,),
    )
    returned_out = exchange_two(hold(out_two, (here,)))
    returned_last = exchange_one(hold(back_one, (returned_out,)))

    (on_down,) = call(pass_on, (single,), (add_down, x_step(far_down, 1)), free=(1,), after=(moved_two,))
    from_next = x_step(near_down, 3)
    from_last = x_step(hold(near_up, (other_core(far_up[:16, :128]),)), 1)
    (on_up,) = call(
        pass_on, (single,), (add_up, x_step(far_up, 3)), free=(1,)
    )
    (result,) = call(result_kernel, (tall,), (target_two, gate_two, returned_out, middle), free=(2,))
    (grad_tokens,) = call(last_kernel, (tall,), (target_one, returned_last, tokens, grad_middle), free=(1,))
    share_down, share_up = call(
        last_sums, (single, single),
        (own_down, from_next, x_step(on_down, 1), own_up, from_last, x_step(on_up, 3)),
        free=(1, 2, 4, 5), after=(result, grad_tokens, grad_up_two, grad_down_two), ahead=6,
    )
    return (
        result,
        grad_tokens,
        share_up[None],
        share_down[None],
        grad_up_two[None],
        grad_down_two[None],
    )


def solution(mesh):
    fine = Mesh(mesh.devices.reshape(2, 4, 2, 2, 4), AXES)
    rows = P(AXES, None)
    weights = P(AXES, None, None)
    return jax.shard_map(
        per_device,
        mesh=fine,
        in_specs=(
            rows, rows, rows, rows, P(AXES), P(AXES), rows, rows,
            P(EX, None, None), P(EX, None, None), weights, weights,
        ),
        out_specs=(rows, rows, P(EX, EY, None), P(EX, EY, None), weights, weights),
        check_vma=False,
    )
```
